128 devices in a mesh: row: 8 (over y, core), col: 16 (over x, z).
Axes of the slice: x: 4, y: 4, z: 4, core: 2. Of those that a mesh axis runs over, the one named last changes fastest.
Arguments:
- embeddings: float32 [131072, 1024], P(('row', 'col')), may hold values from -6 to 6
- neighbour_ids: int32 [256, 12], P(('row', 'col')), may hold values from 0 to 255, as said below
- start_vectors: float32 [131072, 64], P(('row', 'col')), may hold values from -15 to 15
Outputs:
- spectral_vectors: float32 [131072, 64], P(('row', 'col'))
The draws below stay inside these ranges and needn't reach their ends.
Inputs may be any that keep to these rules, and one draw needn't show every extreme that they name: `neighbour_ids`: slot 0 of block b is b itself. The other slots of block b name distinct blocks other than b held by devices of the same row index whose col index differs from that of b's device by at most 2 cyclically, followed by padding slots that repeat b. Block b sits on device b // 2, with device index row * 16 + col.
All inputs are finite; a program needn't handle non-finite values.
Results may differ from the reference program's by a relative error of at most 0.005.
Values may be sent and summed in bfloat16 or wider, within the bound.
A program may use at most 128 MiB of HBM per device.

```python
import math
import jax
import jax.numpy as jnp
from jax import lax

D = 1024
BS = 512
SLOTS = 12
K = 64
REACH = 2
ITERS = 3
BLK_DEV = 2
NBLK = 256
NPTS = 131072
N_ROW = 8
N_COL = 16
DEVICES = 128


def draw_embeddings(key, part):
    per_unit = D // 4
    cycle_topics = N_COL * per_unit
    side_topics = 4
    bump_width = 1.5
    row_ids = jnp.arange(NPTS, dtype=jnp.int32)
    holder = row_ids // (BLK_DEV * BS)
    row_of = holder // N_COL
    col_of = holder % N_COL
    topics = jax.random.normal(jax.random.fold_in(key, 21), (N_ROW * cycle_topics, D), jnp.float32)
    anchor = (col_of - 1) * per_unit + jax.random.randint(jax.random.fold_in(key, 22), (NPTS,), 0, 3 * per_unit)
    offset = jax.random.uniform(jax.random.fold_in(key, 23), (NPTS,), jnp.float32, 0.0, 1.0)
    gain_draws = jax.random.uniform(jax.random.fold_in(key, 24), (NPTS, 2 * side_topics + 1), jnp.float32, 0.6, 1.4)
    noise_scale = jax.random.uniform(jax.random.fold_in(key, 25), (NPTS, 1), jnp.float32, 0.25, 0.35)
    noise_draws = jax.random.normal(jax.random.fold_in(key, 26), (NPTS, D), jnp.float32)
    mixture = jnp.zeros((NPTS, D), jnp.float32)
    energy = jnp.zeros((NPTS, 1), jnp.float32)
    for topic_step in range(-side_topics, side_topics + 1):
        topic_index = (row_of * cycle_topics + (anchor + topic_step + cycle_topics) % cycle_topics).astype(jnp.int32)
        distance = topic_step - offset
        weight = (jnp.exp(-distance * distance / (2.0 * bump_width * bump_width)) * gain_draws[:, topic_step + side_topics])[:, None]
        mixture = mixture + weight * topics[topic_index]
        energy = energy + weight * weight
    mixture = mixture / jnp.sqrt(energy) + noise_scale * noise_draws
    mixture = mixture / jnp.sqrt(1.0 + noise_scale * noise_scale)
    return jnp.clip(mixture, -6.0, 6.0)


def draw_neighbour_ids(key, part):
    blocks = jnp.arange(NBLK, dtype=jnp.int32)
    holder = blocks // BLK_DEV
    row_of = holder // N_COL
    col_of = holder % N_COL
    shifts = jnp.repeat(jnp.arange(-REACH, REACH + 1, dtype=jnp.int32), BLK_DEV)
    within = jnp.tile(jnp.arange(BLK_DEV, dtype=jnp.int32), 2 * REACH + 1)
    cand_ids = (row_of[:, None] * N_COL + (col_of[:, None] + shifts[None, :] + N_COL) % N_COL) * BLK_DEV + within[None, :]
    cand_count = (2 * REACH + 1) * BLK_DEV
    scores = jax.random.randint(jax.random.fold_in(key, 1), (NBLK, cand_count), 0, 1 << 20) * cand_count + jnp.arange(cand_count, dtype=jnp.int32)[None, :]
    scores = jnp.where(cand_ids == blocks[:, None], 1 << 30, scores)
    ranking = jnp.argsort(scores, axis=1, stable=True)
    spaces = min(cand_count - 1, SLOTS - 1)
    ranked = jnp.take_along_axis(cand_ids, ranking, axis=1)[:, :spaces]
    device_level = jax.random.randint(jax.random.fold_in(key, 2), (NBLK // BLK_DEV,), 0, 4)
    jitter = jax.random.randint(jax.random.fold_in(key, 3), (NBLK,), 0, 3)
    listed = jnp.clip(1 + 3 * jnp.repeat(device_level, BLK_DEV) + jitter, 1, spaces)
    listed = listed.at[0].set(spaces)
    listed_ids = jnp.where(jnp.arange(spaces)[None, :] < listed[:, None], ranked, blocks[:, None])
    padding = jnp.broadcast_to(blocks[:, None], (NBLK, SLOTS - 1 - spaces))
    return jnp.concatenate([blocks[:, None], listed_ids, padding], axis=1).astype(jnp.int32)


def draw_start_vectors(key, part):
    row_ids = jnp.arange(NPTS, dtype=jnp.int32)
    device_rise = 1.0 + 2.0 * (row_ids // (BLK_DEV * BS)).astype(jnp.float32) / max(DEVICES - 1, 1)
    values = jnp.clip(jax.random.normal(key, (NPTS, K), jnp.float32), -5.0, 5.0)
    return values * device_rise[:, None]


def setup_inputs(seed: int = 0) -> dict:
    splits = jax.random.split(jax.random.key(seed), 4)
    return {
        "embeddings": draw_embeddings(jax.random.fold_in(splits[3], 71), 0),
        "neighbour_ids": draw_neighbour_ids(jax.random.fold_in(splits[3], 71), 0),
        "start_vectors": draw_start_vectors(jax.random.fold_in(splits[3], 71), 0),
    }


SHARP = 8.0
EPSILON = 1e-06

def unit_rows(points):
    rms_inverse = lax.rsqrt(lax.optimization_barrier(jnp.mean(points * points, axis=-1, keepdims=True)) + EPSILON)
    return (points * rms_inverse).astype(jnp.bfloat16)

def orthonormal(image_rows, total_rows):
    gram_sum = lax.dot_general(image_rows.astype(jnp.float32), image_rows.astype(jnp.float32), (((0,), (0,)), ((), ())), precision=lax.Precision.HIGHEST, preferred_element_type=jnp.float32)
    factor = jnp.linalg.cholesky(gram_sum)
    solved = lax.linalg.triangular_solve(factor, image_rows, left_side=False, lower=True, transpose_a=True)
    return solved * math.sqrt(total_rows)

def reference(embeddings, neighbour_ids, start_vectors):
    block_count = neighbour_ids.shape[0]
    normed = unit_rows(embeddings).reshape(block_count, BS, D)
    block_ids = jnp.arange(block_count, dtype=jnp.int32)
    slot_ids = jnp.arange(SLOTS, dtype=jnp.int32)
    live_mask = ((slot_ids[None, :] == 0) | (neighbour_ids != block_ids[:, None])).astype(jnp.float32)

    def tiles_of(packed):
        own_rows, block_list, live_rows = packed
        nearby = normed[block_list].astype(jnp.float32)
        cosine = jnp.einsum('pd,kqd->kpq', own_rows.astype(jnp.float32), nearby) / D
        affinity = jnp.exp(SHARP * (cosine - 1.0)) * live_rows[:, None, None]
        degree = lax.optimization_barrier(jnp.sum(affinity, axis=(0, 2)))
        return (affinity.astype(jnp.bfloat16), degree)
    tile_rows, degree = lax.map(tiles_of, (normed, neighbour_ids, live_mask))
    inv_root = lax.rsqrt(degree)
    vectors = start_vectors
    for iteration in range(ITERS):
        scaled = (vectors * inv_root.reshape(-1, 1)).astype(jnp.bfloat16).reshape(block_count, BS, K)

        def apply(packed):
            tile_block, block_list, root_rows = packed
            nearby = scaled[block_list].astype(jnp.float32)
            return jnp.einsum('kpq,kqc->pc', tile_block.astype(jnp.float32), nearby) * root_rows[:, None]
        image_rows = lax.map(apply, (tile_rows, neighbour_ids, inv_root)).reshape(-1, K)
        vectors = orthonormal(image_rows, NPTS)
    return vectors
```

```python
import functools
import math

import jax
import jax.numpy as jnp
from jax import lax
from jax.experimental import pallas as pl
from jax.experimental.pallas import tpu as pltpu
from jax.sharding import PartitionSpec as P

D = 1024
BS = 512
SLOTS = 12
K = 64
REACH = 2
ITERS = 3
BLK_DEV = 2
PTS = BS * BLK_DEV
SHARP = 8.0
EPSILON = 1e-06
CORES = 2
Z_CHIPS = 4
MESH = pl.DeviceIdType.MESH
BF16 = jnp.bfloat16
F32 = jnp.float32

CHUNKS = ((0, 256), (256, 256), (512, 256), (768, 256))
PARTIAL = BF16
HALF = PTS // 2
OO, PO, OP, NP, PN = range(5)
OWN, PREV, NEXT = range(3)


def split_hi_lo(x):
    hi = x.astype(BF16)
    return hi, (x - hi.astype(F32)).astype(BF16)


def gram_packed(image):
    hi, lo = split_hi_lo(image)
    both = jnp.concatenate([hi, lo], axis=0)
    full = lax.dot_general(both, both, (((1,), (1,)), ((), ())), preferred_element_type=F32)
    top = full[:K] + full[K:]
    gram = top[:, :K] + top[:, K:]
    return jnp.concatenate([gram[: K // 2], gram[K // 2 :]], axis=1)


def inverse_factor(packed):
    gram = jnp.concatenate([packed[:, :K], packed[:, K:]], axis=0)
    row_ids = lax.broadcasted_iota(jnp.int32, (K, K), 0)
    col_ids = lax.broadcasted_iota(jnp.int32, (K, K), 1)
    eye = jnp.where(row_ids == col_ids, 1.0, 0.0).astype(F32)
    work = jnp.concatenate([gram, eye], axis=1)
    in_group = lax.broadcasted_iota(jnp.int32, (8, 2 * K), 0)
    groups = [work[8 * g : 8 * g + 8] for g in range(K // 8)]
    for k in range(0, K, 2):
        first, r = divmod(k, 8)
        head = groups[first]
        one, two = head[r : r + 1], head[r + 1 : r + 2]
        a, b, d = one[:, k : k + 1], one[:, k + 1 : k + 2], two[:, k + 1 : k + 2]
        inv_a = 1.0 / a
        inv_det = 1.0 / (a * d - b * b)
        t_one = (d * inv_det) * one - (b * inv_det) * two
        t_two = (a * inv_det) * two - (b * inv_det) * one
        for g in range(first, K // 8):
            below = groups[g]
            new = below - below[:, k : k + 1] * t_one - below[:, k + 1 : k + 2] * t_two
            if g == first:
                second = two - (b * inv_a) * one
                new = jnp.where(in_group > r + 1, new, jnp.where(in_group == r + 1, second, below))
            groups[g] = new
    work = jnp.concatenate(groups, axis=0)
    pivots = jnp.sum(work[:, :K] * eye, axis=1, keepdims=True)
    return work[:, K:] * lax.rsqrt(pivots)


def apply_factor(inverse, image):
    mh, ml = split_hi_lo(inverse)
    zh, zl = split_hi_lo(image)
    left = jnp.concatenate([mh, mh, ml, ml], axis=1)
    right = jnp.concatenate([zh, zl, zh, zl], axis=0)
    return jnp.dot(left, right, preferred_element_type=F32)


def kernel(
    n_row, n_col,
    emb, ids, start, out,
    stage, normed, tiles, x_rows, own_mask, got_mask, masks, deg, got_deg,
    scaled, got_scaled, part, got_part, gram, got_gram,
    load_sem, x_sem, emb_send, emb_recv, mask_send, mask_recv, deg_send, deg_recv,
    vec_send, vec_recv, part_send, part_recv, gram_send, gram_recv,
):
    row, col = lax.axis_index("row"), lax.axis_index("col")
    prev = (row, lax.rem(col + n_col - 1, n_col))
    nxt = (row, lax.rem(col + 1, n_col))
    n_y, n_x = n_row // CORES, n_col // Z_CHIPS
    y, core = row // CORES, lax.rem(row, CORES)
    x, z = col // Z_CHIPS, lax.rem(col, Z_CHIPS)
    phases = [
        [(y * CORES + (1 - core), col)],
        [(lax.rem(y + k, n_y) * CORES + core, col) for k in range(1, n_y)],
        [(row, lax.rem(x + k, n_x) * Z_CHIPS + z) for k in range(1, n_x)],
        [(row, x * Z_CHIPS + lax.rem(z + k, Z_CHIPS)) for k in range(1, Z_CHIPS)],
    ]
    mirror = [[n - 1 - k for k in range(n)] for n in map(len, phases)]
    base = [sum(len(p) for p in phases[:i]) for i in range(len(phases))]

    loads = []
    for i, (begin, count) in enumerate(CHUNKS):
        load = pltpu.make_async_copy(
            emb.at[pl.ds(begin, count)], stage.at[pl.ds(begin, count)], load_sem.at[i]
        )
        load.start()
        loads.append(load)
    x_load = pltpu.make_async_copy(start, x_rows, x_sem)
    x_load.start()

    barrier = pltpu.get_barrier_semaphore()
    friends = [prev, nxt] + [d for p in phases for d in p]
    for friend in friends:
        pl.semaphore_signal(barrier, inc=1, device_id=friend, device_id_type=MESH)

    lane = lax.broadcasted_iota(jnp.int32, (BLK_DEV, 128), 1)
    holder = col + (lane >> 1) - REACH
    holder = jnp.where(holder < 0, holder + n_col, jnp.where(holder >= n_col, holder - n_col, holder))
    target = (row * n_col + holder) * BLK_DEV + (lane & 1)
    me = (row * n_col + col) * BLK_DEV + lax.broadcasted_iota(jnp.int32, (BLK_DEV, 128), 0)
    count_listed = jnp.zeros((BLK_DEV, 128), F32)
    for slot in range(SLOTS):
        named = ids[:, slot : slot + 1]
        hit = named == target
        if slot:
            hit = hit & (named != me)
        count_listed += jnp.where(hit, 1.0, 0.0)
    own_mask[...] = jnp.zeros((8, 128), F32)
    own_mask[0:BLK_DEV, :] = count_listed

    def normalize(begin, count):
        step = 32

        def some(i, carry):
            rows = pl.ds(begin + i * step, step)
            e = stage[rows, :]
            inv = lax.rsqrt(jnp.mean(e * e, axis=-1, keepdims=True) + EPSILON)
            normed[OWN, rows, :] = (e * inv).astype(BF16)
            return carry

        lax.fori_loop(0, count // step, some, 0)

    def remote(src, dst, send, recv, device):
        return pltpu.make_async_remote_copy(
            src_ref=src, dst_ref=dst, send_sem=send, recv_sem=recv, device_id=device, device_id_type=MESH
        )

    both = ((nxt, 0), (prev, 1))
    moving = [[], []]
    mask_copies = []
    for i, (begin, count) in enumerate(CHUNKS):
        loads[i].wait()
        normalize(begin, count)
        if i == 0:
            pl.semaphore_wait(barrier, len(friends))
            for device, side in both:
                copy = remote(own_mask, got_mask.at[side], mask_send.at[side], mask_recv.at[side], device)
                copy.start()
                mask_copies.append(copy)
        rows = pl.ds(begin, count)
        for device, side in both:
            copy = remote(
                normed.at[OWN, rows],
                normed.at[PREV + side, rows],
                emb_send.at[side, i],
                emb_recv.at[side, i],
                device,
            )
            copy.start()
            moving[side].append(copy)

    first_block = lax.broadcasted_iota(jnp.int32, (1, PTS), 1) < BS

    def spread_mask(tile, listing, candidate):
        for block in range(BLK_DEV):
            at = candidate + block
            masks[pl.ds(2 * tile + block, 1), :] = jnp.where(
                first_block, listing[0:1, at : at + 1], listing[1:2, at : at + 1]
            )

    def offset_at(offset):
        return (offset + REACH) * BLK_DEV

    left = {OO: OWN, PO: PREV, OP: OWN, NP: NEXT, PN: PREV}
    right = {OO: OWN, PO: OWN, OP: PREV, NP: PREV, PN: NEXT}

    def affinity(tile, r0, r_count, c0, c_count):
        a = normed[left[tile], pl.ds(r0, r_count), :]
        b = normed[right[tile], pl.ds(c0, c_count), :]
        product = lax.dot_general(a, b, (((1,), (1,)), ((), ())), preferred_element_type=F32)
        listed = masks[pl.ds(2 * tile + r0 // BS, 1), pl.ds(c0, c_count)]
        value = jnp.exp(product * (SHARP / D) - SHARP) * listed
        tiles[tile, pl.ds(r0, r_count), pl.ds(c0, c_count)] = value.astype(BF16)
        deg[right[tile], :, pl.ds(c0, c_count)] += jnp.sum(
            value.reshape(r_count // 8, 8, c_count), axis=0
        )

    deg[...] = jnp.zeros((3, 8, PTS), F32)
    mine = own_mask[...]
    spread_mask(OO, mine, offset_at(0))
    spread_mask(PO, mine, offset_at(-1))
    for begin, count in CHUNKS:
        affinity(OO, begin, count, 0, PTS)
    x_load.wait()
    x_cols = x_rows[...].T
    for copy in mask_copies:
        copy.wait()
    theirs = got_mask[0]
    spread_mask(OP, theirs, offset_at(1))
    spread_mask(NP, theirs, offset_at(2))
    spread_mask(PN, got_mask[1], offset_at(-2))

    for i, (begin, count) in enumerate(CHUNKS):
        moving[0][i].wait_recv()
        affinity(PO, begin, count, 0, PTS)
        for b0, n0 in CHUNKS:
            affinity(OP, b0, n0, begin, count)
        moving[1][i].wait_recv()
        end = begin + count
        affinity(NP, begin, count, 0, end)
        affinity(PN, begin, count, 0, end)
        for b0, n0 in CHUNKS[:i]:
            affinity(NP, b0, n0, begin, count)
            affinity(PN, b0, n0, begin, count)

    deg_copies = []
    for device, side in both:
        copy = remote(
            deg.at[NEXT - side], got_deg.at[side], deg_send.at[side], deg_recv.at[side], device
        )
        copy.start()
        deg_copies.append(copy)
    for copy in deg_copies:
        copy.wait_recv()
    degree = jnp.sum(deg[OWN] + got_deg[0] + got_deg[1], axis=0, keepdims=True)
    inv_root = lax.rsqrt(degree)

    pending = deg_copies + moving[0] + moving[1]
    sent_only = []

    def product(vectors, tile, c0, c_count):
        return jnp.dot(vectors, tiles[tile, :, pl.ds(c0, c_count)], preferred_element_type=F32)

    def reduce_send(it, phase, packed):
        gram[it, phase] = packed
        copies = []
        for k, device in enumerate(phases[phase]):
            slot = base[phase] + mirror[phase][k]
            copy = remote(
                gram.at[it, phase],
                got_gram.at[it, slot],
                gram_send.at[it, base[phase] + k],
                gram_recv.at[it, slot],
                device,
            )
            copy.start()
            copies.append(copy)
        sent_only.extend(copies)
        return copies

    def reduce_wait(it, phase, packed, copies):
        for copy in copies:
            copy.wait_recv()
        for k in range(len(phases[phase])):
            packed = packed + got_gram[it, base[phase] + k]
        return packed

    def no_beside(stage_index):
        return None

    def apply_affinity(it, vectors, beside):
        own_scaled = (vectors * inv_root).astype(BF16)
        scaled[it] = own_scaled
        copies = []
        for device, side in both:
            copy = remote(
                scaled.at[it], got_scaled.at[it, side], vec_send.at[it, side], vec_recv.at[it, side], device
            )
            copy.start()
            copies.append(copy)
        sent_only.extend(copies)
        beside(0)
        total = product(own_scaled, OO, 0, PTS)
        to_prev = product(own_scaled, OP, 0, PTS)
        beside(1)
        copies[0].wait_recv()
        copies[1].wait_recv()
        from_prev, from_next = got_scaled[it, 0], got_scaled[it, 1]
        part_copies = []
        for half in range(2):
            at = pl.ds(half * HALF, HALF)
            for device, side in both:
                if side == 0:
                    piece = product(from_prev, PN, half * HALF, HALF)
                else:
                    piece = to_prev[:, half * HALF : (half + 1) * HALF]
                    piece = piece + product(from_next, NP, half * HALF, HALF)
                part[it, side, half] = piece.astype(PARTIAL)
                copy = remote(
                    part.at[it, side, half],
                    got_part.at[it, side, half],
                    part_send.at[it, side, half],
                    part_recv.at[it, side, half],
                    device,
                )
                copy.start()
                part_copies.append(copy)
        sent_only.extend(part_copies)
        beside(2)
        total = total + product(from_prev, PO, 0, PTS)
        beside(3)
        for copy in part_copies:
            copy.wait_recv()
        halves = [
            got_part[it, 0, half].astype(F32) + got_part[it, 1, half].astype(F32) for half in range(2)
        ]
        return (total + jnp.concatenate(halves, axis=1)) * inv_root

    scale = math.sqrt(n_row * n_col * PTS)
    image = apply_affinity(0, x_cols, no_beside)
    for it in range(1, ITERS):
        state = {}

        def beside(stage_index):
            if stage_index == 0:
                state["sum"] = gram_packed(image)
            else:
                state["sum"] = reduce_wait(it - 1, stage_index - 1, state["sum"], state["copies"])
            if stage_index < len(phases):
                state["copies"] = reduce_send(it - 1, stage_index, state["sum"])

        following = apply_affinity(it, image, beside)
        beside(4)
        factor = inverse_factor(state["sum"]) * scale
        image = apply_factor(factor, following)

    packed = gram_packed(image)
    for phase in range(len(phases)):
        copies = reduce_send(ITERS - 1, phase, packed)
        packed = reduce_wait(ITERS - 1, phase, packed, copies)
    result = apply_factor(inverse_factor(packed) * scale, image)
    out[...] = result.T

    for copy in pending + sent_only:
        copy.wait_send()


def on_device(n_row, n_col, embeddings, neighbour_ids, start_vectors):
    sums = 1 + (n_row // CORES - 1) + (n_col // Z_CHIPS - 1) + (Z_CHIPS - 1)
    n_chunks = len(CHUNKS)
    return pl.pallas_call(
        functools.partial(kernel, n_row, n_col),
        out_shape=jax.ShapeDtypeStruct((PTS, K), F32),
        in_specs=[
            pl.BlockSpec(memory_space=pl.ANY),
            pl.BlockSpec(memory_space=pltpu.VMEM),
            pl.BlockSpec(memory_space=pl.ANY),
        ],
        out_specs=pl.BlockSpec(memory_space=pltpu.VMEM),
        scratch_shapes=[
            pltpu.VMEM((PTS, D), F32),
            pltpu.VMEM((3, PTS, D), BF16),
            pltpu.VMEM((5, PTS, PTS), BF16),
            pltpu.VMEM((PTS, K), F32),
            pltpu.VMEM((8, 128), F32),
            pltpu.VMEM((2, 8, 128), F32),
            pltpu.VMEM((16, PTS), F32),
            pltpu.VMEM((3, 8, PTS), F32),
            pltpu.VMEM((2, 8, PTS), F32),
            pltpu.VMEM((ITERS, K, PTS), BF16),
            pltpu.VMEM((ITERS, 2, K, PTS), BF16),
            pltpu.VMEM((ITERS, 2, 2, K, HALF), PARTIAL),
            pltpu.VMEM((ITERS, 2, 2, K, HALF), PARTIAL),
            pltpu.VMEM((ITERS, 4, K // 2, 2 * K), F32),
            pltpu.VMEM((ITERS, sums, K // 2, 2 * K), F32),
            pltpu.SemaphoreType.DMA((n_chunks,)),
            pltpu.SemaphoreType.DMA,
            pltpu.SemaphoreType.DMA((2, n_chunks)),
            pltpu.SemaphoreType.DMA((2, n_chunks)),
            pltpu.SemaphoreType.DMA((2,)),
            pltpu.SemaphoreType.DMA((2,)),
            pltpu.SemaphoreType.DMA((2,)),
            pltpu.SemaphoreType.DMA((2,)),
            pltpu.SemaphoreType.DMA((ITERS, 2)),
            pltpu.SemaphoreType.DMA((ITERS, 2)),
            pltpu.SemaphoreType.DMA((ITERS, 2, 2)),
            pltpu.SemaphoreType.DMA((ITERS, 2, 2)),
            pltpu.SemaphoreType.DMA((ITERS, sums)),
            pltpu.SemaphoreType.DMA((ITERS, sums)),
        ],
        compiler_params=pltpu.CompilerParams(
            collective_id=0, has_side_effects=True, vmem_limit_bytes=48 * 2**20
        ),
    )(embeddings, neighbour_ids, start_vectors)


def solution(mesh):
    split = P(("row", "col"), None)
    return jax.shard_map(
        functools.partial(on_device, mesh.shape["row"], mesh.shape["col"]),
        mesh=mesh,
        in_specs=(split, split, split),
        out_specs=split,
        check_vma=False,
    )
```

```python
import functools
import math

import jax
import jax.numpy as jnp
from jax import lax
from jax.experimental import pallas as pl
from jax.experimental.pallas import tpu as pltpu
from jax.sharding import PartitionSpec as P

D = 1024
BS = 512
SLOTS = 12
K = 64
REACH = 2
ITERS = 3
BLK_DEV = 2
PTS = BS * BLK_DEV
SHARP = 8.0
EPSILON = 1e-06
CORES = 2
Z_CHIPS = 4
MESH = pl.DeviceIdType.MESH
BF16 = jnp.bfloat16
F32 = jnp.float32

CHUNKS = ((0, 256), (256, 256), (512, 256), (768, 128), (896, 128))
PARTIAL = BF16
HALF = PTS // 2
OO, PO, OP, NP, PN = range(5)
OWN, PREV, NEXT = range(3)


def split_hi_lo(x):
    hi = x.astype(BF16)
    return hi, (x - hi.astype(F32)).astype(BF16)


def gram_packed(image):
    hi, lo = split_hi_lo(image)
    both = jnp.concatenate([hi, lo], axis=0)
    full = lax.dot_general(both, both, (((1,), (1,)), ((), ())), preferred_element_type=F32)
    top = full[:K] + full[K:]
    gram = top[:, :K] + top[:, K:]
    return jnp.concatenate([gram[: K // 2], gram[K // 2 :]], axis=1)


def inverse_factor(packed):
    gram = jnp.concatenate([packed[:, :K], packed[:, K:]], axis=0)
    row_ids = lax.broadcasted_iota(jnp.int32, (K, K), 0)
    col_ids = lax.broadcasted_iota(jnp.int32, (K, K), 1)
    eye = jnp.where(row_ids == col_ids, 1.0, 0.0).astype(F32)
    work = jnp.concatenate([gram, eye], axis=1)
    in_group = lax.broadcasted_iota(jnp.int32, (8, 2 * K), 0)
    groups = [work[8 * g : 8 * g + 8] for g in range(K // 8)]
    for k in range(0, K, 2):
        first, r = divmod(k, 8)
        head = groups[first]
        one, two = head[r : r + 1], head[r + 1 : r + 2]
        a, b, d = one[:, k : k + 1], one[:, k + 1 : k + 2], two[:, k + 1 : k + 2]
        inv_a = 1.0 / a
        inv_det = 1.0 / (a * d - b * b)
        t_one = (d * inv_det) * one - (b * inv_det) * two
        t_two = (a * inv_det) * two - (b * inv_det) * one
        for g in range(first, K // 8):
            below = groups[g]
            new = below - below[:, k : k + 1] * t_one - below[:, k + 1 : k + 2] * t_two
            if g == first:
                second = two - (b * inv_a) * one
                new = jnp.where(in_group > r + 1, new, jnp.where(in_group == r + 1, second, below))
            groups[g] = new
    work = jnp.concatenate(groups, axis=0)
    pivots = jnp.sum(work[:, :K] * eye, axis=1, keepdims=True)
    return work[:, K:] * lax.rsqrt(pivots)


def apply_factor(inverse, image):
    mh, ml = split_hi_lo(inverse)
    zh, zl = split_hi_lo(image)
    left = jnp.concatenate([mh, mh, ml, ml], axis=1)
    right = jnp.concatenate([zh, zl, zh, zl], axis=0)
    return jnp.dot(left, right, preferred_element_type=F32)


def kernel(
    n_row, n_col,
    emb, ids_given, start, out,
    stage, normed, tiles, x_cols, ids, own_mask, got_mask, masks, deg, got_deg,
    scaled, got_scaled, part, got_part, gram, got_gram,
    load_sem, x_sem, emb_send, emb_recv, mask_send, mask_recv, deg_send, deg_recv,
    vec_send, vec_recv, part_send, part_recv, gram_send, gram_recv,
):
    row, col = lax.axis_index("row"), lax.axis_index("col")
    prev = (row, lax.rem(col + n_col - 1, n_col))
    nxt = (row, lax.rem(col + 1, n_col))
    n_y, n_x = n_row // CORES, n_col // Z_CHIPS
    y, core = row // CORES, lax.rem(row, CORES)
    x, z = col // Z_CHIPS, lax.rem(col, Z_CHIPS)
    steps = [
        [(a, b) for a in range(n_y) for b in range(CORES) if a or b],
        [(a, b) for a in range(n_x) for b in range(Z_CHIPS) if a or b],
    ]
    phases = [
        [(lax.rem(y + a, n_y) * CORES + lax.rem(core + b, CORES), col) for a, b in steps[0]],
        [(row, lax.rem(x + a, n_x) * Z_CHIPS + lax.rem(z + b, Z_CHIPS)) for a, b in steps[1]],
    ]
    mirror = [
        [steps[0].index((-a % n_y, -b % CORES)) for a, b in steps[0]],
        [steps[1].index((-a % n_x, -b % Z_CHIPS)) for a, b in steps[1]],
    ]
    base = [0, len(steps[0])]

    loads = []
    for i, (begin, count) in enumerate(CHUNKS):
        load = pltpu.make_async_copy(
            emb.at[pl.ds(begin, count)], stage.at[pl.ds(begin, count)], load_sem.at[i]
        )
        load.start()
        loads.append(load)
    x_load = pltpu.make_async_copy(start, x_cols, x_sem.at[0])
    x_load.start()
    ids_load = pltpu.make_async_copy(ids_given, ids, x_sem.at[1])
    ids_load.start()

    barrier = pltpu.get_barrier_semaphore()
    friends = [d for p in phases for d in p]
    for friend in friends:
        pl.semaphore_signal(barrier, inc=1, device_id=friend, device_id_type=MESH)

    lane = lax.broadcasted_iota(jnp.int32, (BLK_DEV, 128), 1)
    holder = col + (lane >> 1) - REACH
    holder = jnp.where(holder < 0, holder + n_col, jnp.where(holder >= n_col, holder - n_col, holder))
    target = (row * n_col + holder) * BLK_DEV + (lane & 1)
    me = (row * n_col + col) * BLK_DEV + lax.broadcasted_iota(jnp.int32, (BLK_DEV, 128), 0)
    ids_load.wait()
    count_listed = jnp.zeros((BLK_DEV, 128), F32)
    for slot in range(SLOTS):
        named = ids[:, slot : slot + 1]
        hit = named == target
        if slot:
            hit = hit & (named != me)
        count_listed += jnp.where(hit, 1.0, 0.0)
    own_mask[...] = jnp.zeros((8, 128), F32)
    own_mask[0:BLK_DEV, :] = count_listed

    def normalize(begin, count):
        step = 32

        def some(i, carry):
            rows = pl.ds(begin + i * step, step)
            e = stage[rows, :]
            inv = lax.rsqrt(jnp.mean(e * e, axis=-1, keepdims=True) + EPSILON)
            normed[OWN, rows, :] = (e * inv).astype(BF16)
            return carry

        lax.fori_loop(0, count // step, some, 0)

    def remote(src, dst, send, recv, device):
        return pltpu.make_async_remote_copy(
            src_ref=src, dst_ref=dst, send_sem=send, recv_sem=recv, device_id=device, device_id_type=MESH
        )

    both = ((nxt, 0), (prev, 1))
    moving = [[], []]
    mask_copies = []
    for i, (begin, count) in enumerate(CHUNKS):
        loads[i].wait()
        normalize(begin, count)
        if i == 0:
            pl.semaphore_wait(barrier, len(friends))
            for device, side in both:
                copy = remote(own_mask, got_mask.at[side], mask_send.at[side], mask_recv.at[side], device)
                copy.start()
                mask_copies.append(copy)
        rows = pl.ds(begin, count)
        for device, side in both:
            copy = remote(
                normed.at[OWN, rows],
                normed.at[PREV + side, rows],
                emb_send.at[side, i],
                emb_recv.at[side, i],
                device,
            )
            copy.start()
            moving[side].append(copy)

    first_block = lax.broadcasted_iota(jnp.int32, (1, PTS), 1) < BS

    def spread_mask(tile, listing, candidate):
        for block in range(BLK_DEV):
            at = candidate + block
            masks[pl.ds(2 * tile + block, 1), :] = jnp.where(
                first_block, listing[0:1, at : at + 1], listing[1:2, at : at + 1]
            )

    def offset_at(offset):
        return (offset + REACH) * BLK_DEV

    left = {OO: OWN, PO: PREV, OP: OWN, NP: NEXT, PN: PREV}
    right = {OO: OWN, PO: OWN, OP: PREV, NP: PREV, PN: NEXT}

    def affinity(tile, r0, r_count, c0, c_count):
        a = normed[left[tile], pl.ds(r0, r_count), :]
        b = normed[right[tile], pl.ds(c0, c_count), :]
        product = lax.dot_general(a, b, (((1,), (1,)), ((), ())), preferred_element_type=F32)
        listed = masks[pl.ds(2 * tile + r0 // BS, 1), pl.ds(c0, c_count)]
        value = jnp.exp(product * (SHARP / D) - SHARP) * listed
        tiles[tile, pl.ds(r0, r_count), pl.ds(c0, c_count)] = value.astype(BF16)
        deg[right[tile], :, pl.ds(c0, c_count)] += jnp.sum(
            value.reshape(r_count // 8, 8, c_count), axis=0
        )

    deg[...] = jnp.zeros((3, 8, PTS), F32)
    mine = own_mask[...]
    spread_mask(OO, mine, offset_at(0))
    spread_mask(PO, mine, offset_at(-1))
    for begin, count in CHUNKS:
        affinity(OO, begin, count, 0, PTS)
    x_load.wait()
    for copy in mask_copies:
        copy.wait()
    theirs = got_mask[0]
    spread_mask(OP, theirs, offset_at(1))
    spread_mask(NP, theirs, offset_at(2))
    spread_mask(PN, got_mask[1], offset_at(-2))

    for i, (begin, count) in enumerate(CHUNKS):
        moving[0][i].wait_recv()
        affinity(PO, begin, count, 0, PTS)
        for b0, n0 in CHUNKS:
            affinity(OP, b0, n0, begin, count)
        moving[1][i].wait_recv()
        end = begin + count
        affinity(NP, begin, count, 0, end)
        affinity(PN, begin, count, 0, end)
        for b0, n0 in CHUNKS[:i]:
            affinity(NP, b0, n0, begin, count)
            affinity(PN, b0, n0, begin, count)

    deg_copies = []
    for device, side in both:
        copy = remote(
            deg.at[NEXT - side], got_deg.at[side], deg_send.at[side], deg_recv.at[side], device
        )
        copy.start()
        deg_copies.append(copy)
    for copy in deg_copies:
        copy.wait_recv()
    degree = jnp.sum(deg[OWN] + got_deg[0] + got_deg[1], axis=0, keepdims=True)
    inv_root = lax.rsqrt(degree)

    pending = deg_copies + moving[0] + moving[1]
    sent_only = []

    def product(vectors, tile, c0, c_count):
        return jnp.dot(vectors, tiles[tile, :, pl.ds(c0, c_count)], preferred_element_type=F32)

    def reduce_send(it, phase, packed):
        gram[it, phase] = packed
        copies = []
        for k, device in enumerate(phases[phase]):
            slot = base[phase] + mirror[phase][k]
            copy = remote(
                gram.at[it, phase],
                got_gram.at[it, slot],
                gram_send.at[it, base[phase] + k],
                gram_recv.at[it, slot],
                device,
            )
            copy.start()
            copies.append(copy)
        sent_only.extend(copies)
        return copies

    def reduce_wait(it, phase, packed, copies):
        for copy in copies:
            copy.wait_recv()
        for k in range(len(phases[phase])):
            packed = packed + got_gram[it, base[phase] + k]
        return packed

    def no_beside(stage_index):
        return None

    def apply_affinity(it, vectors, beside):
        beside(0)
        own_scaled = (vectors * inv_root).astype(BF16)
        scaled[it] = own_scaled
        copies = []
        for device, side in both:
            copy = remote(
                scaled.at[it], got_scaled.at[it, side], vec_send.at[it, side], vec_recv.at[it, side], device
            )
            copy.start()
            copies.append(copy)
        sent_only.extend(copies)
        total = product(own_scaled, OO, 0, PTS)
        to_prev = product(own_scaled, OP, 0, PTS)
        beside(1)
        copies[0].wait_recv()
        copies[1].wait_recv()
        from_prev, from_next = got_scaled[it, 0], got_scaled[it, 1]
        part_copies = []
        for half in range(2):
            at = pl.ds(half * HALF, HALF)
            for device, side in both:
                if side == 0:
                    piece = product(from_prev, PN, half * HALF, HALF)
                else:
                    piece = to_prev[:, half * HALF : (half + 1) * HALF]
                    piece = piece + product(from_next, NP, half * HALF, HALF)
                part[it, side, half] = piece.astype(PARTIAL)
                copy = remote(
                    part.at[it, side, half],
                    got_part.at[it, side, half],
                    part_send.at[it, side, half],
                    part_recv.at[it, side, half],
                    device,
                )
                copy.start()
                part_copies.append(copy)
        sent_only.extend(part_copies)
        total = total + product(from_prev, PO, 0, PTS)
        beside(2)
        for copy in part_copies:
            copy.wait_recv()
        halves = [
            got_part[it, 0, half].astype(F32) + got_part[it, 1, half].astype(F32) for half in range(2)
        ]
        return (total + jnp.concatenate(halves, axis=1)) * inv_root

    scale = math.sqrt(n_row * n_col * PTS)
    image = apply_affinity(0, x_cols[...], no_beside)
    for it in range(1, ITERS):
        state = {}

        def beside(stage_index):
            if stage_index == 0:
                state["sum"] = gram_packed(image)
            else:
                state["sum"] = reduce_wait(it - 1, stage_index - 1, state["sum"], state["copies"])
            if stage_index < len(phases):
                state["copies"] = reduce_send(it - 1, stage_index, state["sum"])
            else:
                state["factor"] = inverse_factor(state["sum"]) * scale

        following = apply_affinity(it, image, beside)
        image = apply_factor(state["factor"], following)

    packed = gram_packed(image)
    for phase in range(len(phases)):
        copies = reduce_send(ITERS - 1, phase, packed)
        packed = reduce_wait(ITERS - 1, phase, packed, copies)
    result = apply_factor(inverse_factor(packed) * scale, image)
    out[...] = result

    for copy in pending + sent_only:
        copy.wait_send()


def on_device(n_row, n_col, embeddings, neighbour_ids, start_vectors):
    sums = n_row - 1 + n_col - 1
    n_chunks = len(CHUNKS)
    return pl.pallas_call(
        functools.partial(kernel, n_row, n_col),
        out_shape=jax.ShapeDtypeStruct((K, PTS), F32),
        in_specs=[
            pl.BlockSpec(memory_space=pl.ANY),
            pl.BlockSpec(memory_space=pl.ANY),
            pl.BlockSpec(memory_space=pl.ANY),
        ],
        out_specs=pl.BlockSpec(memory_space=pltpu.VMEM),
        scratch_shapes=[
            pltpu.VMEM((PTS, D), F32),
            pltpu.VMEM((3, PTS, D), BF16),
            pltpu.VMEM((5, PTS, PTS), BF16),
            pltpu.VMEM((K, PTS), F32),
            pltpu.VMEM((BLK_DEV, SLOTS), jnp.int32),
            pltpu.VMEM((8, 128), F32),
            pltpu.VMEM((2, 8, 128), F32),
            pltpu.VMEM((16, PTS), F32),
            pltpu.VMEM((3, 8, PTS), F32),
            pltpu.VMEM((2, 8, PTS), F32),
            pltpu.VMEM((ITERS, K, PTS), BF16),
            pltpu.VMEM((ITERS, 2, K, PTS), BF16),
            pltpu.VMEM((ITERS, 2, 2, K, HALF), PARTIAL),
            pltpu.VMEM((ITERS, 2, 2, K, HALF), PARTIAL),
            pltpu.VMEM((ITERS, 2, K // 2, 2 * K), F32),
            pltpu.VMEM((ITERS, sums, K // 2, 2 * K), F32),
            pltpu.SemaphoreType.DMA((n_chunks,)),
            pltpu.SemaphoreType.DMA((2,)),
            pltpu.SemaphoreType.DMA((2, n_chunks)),
            pltpu.SemaphoreType.DMA((2, n_chunks)),
            pltpu.SemaphoreType.DMA((2,)),
            pltpu.SemaphoreType.DMA((2,)),
            pltpu.SemaphoreType.DMA((2,)),
            pltpu.SemaphoreType.DMA((2,)),
            pltpu.SemaphoreType.DMA((ITERS, 2)),
            pltpu.SemaphoreType.DMA((ITERS, 2)),
            pltpu.SemaphoreType.DMA((ITERS, 2, 2)),
            pltpu.SemaphoreType.DMA((ITERS, 2, 2)),
            pltpu.SemaphoreType.DMA((ITERS, sums)),
            pltpu.SemaphoreType.DMA((ITERS, sums)),
        ],
        compiler_params=pltpu.CompilerParams(
            collective_id=0, has_side_effects=True, vmem_limit_bytes=63 * 2**20
        ),
    )(embeddings, neighbour_ids, start_vectors.T).T


def solution(mesh):
    split = P(("row", "col"), None)
    return jax.shard_map(
        functools.partial(on_device, mesh.shape["row"], mesh.shape["col"]),
        mesh=mesh,
        in_specs=(split, split, split),
        out_specs=split,
        check_vma=False,
    )
```

```python
import functools
import math

import jax
import jax.numpy as jnp
from jax import lax
from jax.experimental import pallas as pl
from jax.experimental.pallas import tpu as pltpu
from jax.sharding import PartitionSpec as P

D = 1024
BS = 512
SLOTS = 12
K = 64
REACH = 2
ITERS = 3
BLK_DEV = 2
PTS = BS * BLK_DEV
SHARP = 8.0
EPSILON = 1e-06
CORES = 2
Z_CHIPS = 4
MESH = pl.DeviceIdType.MESH
BF16 = jnp.bfloat16
F32 = jnp.float32

CHUNKS = ((0, 256), (256, 256), (512, 256), (768, 128), (896, 128))
PARTIAL = BF16
HALF = PTS // 2
OO, PO, OP, NP, PN = range(5)
OWN, PREV, NEXT = range(3)


def split_hi_lo(x):
    hi = x.astype(BF16)
    return hi, (x - hi.astype(F32)).astype(BF16)


def gram_packed(image):
    hi, lo = split_hi_lo(image)
    both = jnp.concatenate([hi, lo], axis=0)
    full = lax.dot_general(both, both, (((1,), (1,)), ((), ())), preferred_element_type=F32)
    top = full[:K] + full[K:]
    gram = top[:, :K] + top[:, K:]
    return jnp.concatenate([gram[: K // 2], gram[K // 2 :]], axis=1)


def inverse_factor(packed):
    gram = jnp.concatenate([packed[:, :K], packed[:, K:]], axis=0)
    row_ids = lax.broadcasted_iota(jnp.int32, (K, K), 0)
    col_ids = lax.broadcasted_iota(jnp.int32, (K, K), 1)
    eye = jnp.where(row_ids == col_ids, 1.0, 0.0).astype(F32)
    work = jnp.concatenate([gram, eye], axis=1)
    in_group = lax.broadcasted_iota(jnp.int32, (8, 2 * K), 0)
    groups = [work[8 * g : 8 * g + 8] for g in range(K // 8)]

    def wide(value):
        return jnp.broadcast_to(value, (8, 2 * K))

    for k in range(0, K, 4):
        first, r = divmod(k, 8)
        head = groups[first]
        rows = [wide(head[r + i : r + i + 1]) for i in range(4)]
        p = {
            (i, j): wide(head[r + i : r + i + 1, k + j : k + j + 1])
            for i in range(4)
            for j in range(i, 4)
        }
        columns = [[wide(group[:, k + i : k + i + 1]) for i in range(4)] for group in groups[first:]]
        a, b, d = p[0, 0], p[0, 1], p[1, 1]
        inv_a = 1.0 / a
        inv_det = 1.0 / (a * d - b * b)
        d_, b_, a_ = d * inv_det, b * inv_det, a * inv_det
        w = {j: (d_ * p[0, j] - b_ * p[1, j], a_ * p[1, j] - b_ * p[0, j]) for j in (2, 3)}
        u0 = d_ * rows[0] - b_ * rows[1]
        u1 = a_ * rows[1] - b_ * rows[0]
        s22 = p[2, 2] - w[2][0] * p[0, 2] - w[2][1] * p[1, 2]
        s23 = p[2, 3] - w[2][0] * p[0, 3] - w[2][1] * p[1, 3]
        s33 = p[3, 3] - w[3][0] * p[0, 3] - w[3][1] * p[1, 3]
        inv_s22 = 1.0 / s22
        inv_rest = 1.0 / (s22 * s33 - s23 * s23)
        s2 = rows[2] - p[0, 2] * u0 - p[1, 2] * u1
        s3 = rows[3] - p[0, 3] * u0 - p[1, 3] * u1
        t2 = (s33 * inv_rest) * s2 - (s23 * inv_rest) * s3
        t3 = (s22 * inv_rest) * s3 - (s23 * inv_rest) * s2
        t0 = u0 - w[2][0] * t2 - w[3][0] * t3
        t1 = u1 - w[2][1] * t2 - w[3][1] * t3
        for g in range(first, K // 8):
            c = columns[g - first]
            below = groups[g]
            new = below - (c[0] * t0 + c[1] * t1) - (c[2] * t2 + c[3] * t3)
            if g == first:
                second = rows[1] - (b * inv_a) * rows[0]
                fourth = s3 - (s23 * inv_s22) * s2
                kept = jnp.where(in_group == r + 2, s2, jnp.where(in_group == r + 3, fourth, below))
                kept = jnp.where(in_group == r + 1, second, kept)
                new = jnp.where(in_group > r + 3, new, kept)
            groups[g] = new
    work = jnp.concatenate(groups, axis=0)
    pivots = jnp.sum(work[:, :K] * eye, axis=1, keepdims=True)
    return work[:, K:] * lax.rsqrt(pivots)


def folded(row):
    return jnp.concatenate([row[:, 128 * g : 128 * g + 128] for g in range(PTS // 128)], axis=0)


def unfolded(tile):
    return jnp.concatenate([tile[g : g + 1] for g in range(PTS // 128)], axis=1)


def apply_factor(inverse, image):
    mh, ml = split_hi_lo(inverse)
    zh, zl = split_hi_lo(image)
    left = jnp.concatenate([mh, mh, ml, ml], axis=1)
    right = jnp.concatenate([zh, zl, zh, zl], axis=0)
    return jnp.dot(left, right, preferred_element_type=F32)


def kernel(
    n_row, n_col,
    emb, ids_given, start, out,
    stage, normed, tiles, x_cols, ids, own_mask, got_mask, masks, deg, deg_sum, near_deg, far_deg,
    x_half, got_x, factors,
    scaled, got_scaled, part, got_part, gram, got_gram,
    load_sem, x_sem, emb_send, emb_recv, mask_send, mask_recv, deg_send, deg_recv, start_send, start_recv,
    vec_send, vec_recv, part_send, part_recv, gram_send, gram_recv,
):
    row, col = lax.axis_index("row"), lax.axis_index("col")
    prev = (row, lax.rem(col + n_col - 1, n_col))
    nxt = (row, lax.rem(col + 1, n_col))
    n_y, n_x = n_row // CORES, n_col // Z_CHIPS
    y, core = row // CORES, lax.rem(row, CORES)
    x, z = col // Z_CHIPS, lax.rem(col, Z_CHIPS)
    steps = [
        [(a, b) for a in range(n_y) for b in range(CORES) if a or b],
        [(a, b) for a in range(n_x) for b in range(Z_CHIPS) if a or b],
    ]
    phases = [
        [(lax.rem(y + a, n_y) * CORES + lax.rem(core + b, CORES), col) for a, b in steps[0]],
        [(row, lax.rem(x + a, n_x) * Z_CHIPS + lax.rem(z + b, Z_CHIPS)) for a, b in steps[1]],
    ]
    mirror = [
        [steps[0].index((-a % n_y, -b % CORES)) for a, b in steps[0]],
        [steps[1].index((-a % n_x, -b % Z_CHIPS)) for a, b in steps[1]],
    ]
    base = [0, len(steps[0])]

    loads = []
    for i, (begin, count) in enumerate(CHUNKS):
        load = pltpu.make_async_copy(
            emb.at[pl.ds(begin, count)], stage.at[pl.ds(begin, count)], load_sem.at[i]
        )
        load.start()
        loads.append(load)
    x_load = pltpu.make_async_copy(start, x_cols, x_sem.at[0])
    x_load.start()
    ids_load = pltpu.make_async_copy(ids_given, ids, x_sem.at[1])
    ids_load.start()

    barrier = pltpu.get_barrier_semaphore()
    friends = [d for p in phases for d in p]
    for friend in friends:
        pl.semaphore_signal(barrier, inc=1, device_id=friend, device_id_type=MESH)

    lane = lax.broadcasted_iota(jnp.int32, (BLK_DEV, 128), 1)
    holder = col + (lane >> 1) - REACH
    holder = jnp.where(holder < 0, holder + n_col, jnp.where(holder >= n_col, holder - n_col, holder))
    target = (row * n_col + holder) * BLK_DEV + (lane & 1)
    me = (row * n_col + col) * BLK_DEV + lax.broadcasted_iota(jnp.int32, (BLK_DEV, 128), 0)
    ids_load.wait()
    count_listed = jnp.zeros((BLK_DEV, 128), F32)
    for slot in range(SLOTS):
        named = ids[:, slot : slot + 1]
        hit = named == target
        if slot:
            hit = hit & (named != me)
        count_listed += jnp.where(hit, 1.0, 0.0)
    own_mask[...] = jnp.zeros((8, 128), F32)
    own_mask[0:BLK_DEV, :] = count_listed

    def normalize(begin, count):
        step = 32

        def some(i, carry):
            rows = pl.ds(begin + i * step, step)
            e = stage[rows, :]
            inv = lax.rsqrt(jnp.mean(e * e, axis=-1, keepdims=True) + EPSILON)
            normed[OWN, rows, :] = (e * inv).astype(BF16)
            return carry

        lax.fori_loop(0, count // step, some, 0)

    def remote(src, dst, send, recv, device):
        return pltpu.make_async_remote_copy(
            src_ref=src, dst_ref=dst, send_sem=send, recv_sem=recv, device_id=device, device_id_type=MESH
        )

    both = ((nxt, 0), (prev, 1))
    moving = [[], []]
    start_copies = []
    mask_copies = []
    for i, (begin, count) in enumerate(CHUNKS):
        loads[i].wait()
        normalize(begin, count)
        if i == 0:
            pl.semaphore_wait(barrier, len(friends))
            for device, side in both:
                copy = remote(own_mask, got_mask.at[side], mask_send.at[side], mask_recv.at[side], device)
                copy.start()
                mask_copies.append(copy)
        rows = pl.ds(begin, count)
        for device, side in both:
            copy = remote(
                normed.at[OWN, rows],
                normed.at[PREV + side, rows],
                emb_send.at[side, i],
                emb_recv.at[side, i],
                device,
            )
            copy.start()
            moving[side].append(copy)
        if i == 0:
            x_load.wait()
            x_half[...] = x_cols[...].astype(BF16)
            for device, side in both:
                copy = remote(x_half, got_x.at[side], start_send.at[side], start_recv.at[side], device)
                copy.start()
                start_copies.append(copy)

    first_block = lax.broadcasted_iota(jnp.int32, (1, PTS), 1) < BS

    def spread_mask(tile, listing, candidate):
        for block in range(BLK_DEV):
            at = candidate + block
            masks[pl.ds(2 * tile + block, 1), :] = jnp.where(
                first_block, listing[0:1, at : at + 1], listing[1:2, at : at + 1]
            )

    def offset_at(offset):
        return (offset + REACH) * BLK_DEV

    left = {OO: OWN, PO: PREV, OP: OWN, NP: NEXT, PN: PREV}
    right = {OO: OWN, PO: OWN, OP: PREV, NP: PREV, PN: NEXT}

    def affinity(tile, r0, r_count, c0, c_count):
        a = normed[left[tile], pl.ds(r0, r_count), :]
        b = normed[right[tile], pl.ds(c0, c_count), :]
        product = lax.dot_general(a, b, (((1,), (1,)), ((), ())), preferred_element_type=F32)
        value = jnp.exp(product * (SHARP / D) - SHARP)
        lists = [masks[pl.ds(2 * tile + block, 1), pl.ds(c0, c_count)] for block in range(BLK_DEV)]
        if r0 < BS < r0 + r_count:
            above = BS - r0
            value = jnp.concatenate([value[:above] * lists[0], value[above:] * lists[1]], axis=0)
        else:
            value = value * lists[r0 // BS]
        tiles[tile, pl.ds(r0, r_count), pl.ds(c0, c_count)] = value.astype(BF16)
        deg[right[tile], :, pl.ds(c0, c_count)] += jnp.sum(
            value.reshape(r_count // 8, 8, c_count), axis=0
        )

    deg[...] = jnp.zeros((3, 8, PTS), F32)
    mine = own_mask[...]
    spread_mask(OO, mine, offset_at(0))
    spread_mask(PO, mine, offset_at(-1))
    for begin, count in CHUNKS:
        affinity(OO, begin, count, 0, PTS)
    for copy in mask_copies:
        copy.wait()
    theirs = got_mask[0]
    spread_mask(OP, theirs, offset_at(1))
    spread_mask(NP, theirs, offset_at(2))
    spread_mask(PN, got_mask[1], offset_at(-2))

    for i, (begin, count) in enumerate(CHUNKS):
        moving[0][i].wait_recv()
        affinity(PO, begin, count, 0, PTS)
        affinity(OP, 0, PTS, begin, count)
        moving[1][i].wait_recv()
        end = begin + count
        affinity(NP, begin, count, 0, end)
        affinity(PN, begin, count, 0, end)
        if begin:
            affinity(NP, 0, begin, begin, count)
            affinity(PN, 0, begin, begin, count)

    for place, where in enumerate((PREV, OWN, NEXT)):
        deg_sum[place] = folded(jnp.sum(deg[where], axis=0, keepdims=True))
    far_prev = (row, lax.rem(col + n_col - 2, n_col))
    far_next = (row, lax.rem(col + 2, n_col))
    deg_copies = [
        remote(deg_sum.at[pl.ds(1, 2)], near_deg.at[0], deg_send.at[0], deg_recv.at[0], nxt),
        remote(deg_sum.at[pl.ds(0, 2)], near_deg.at[1], deg_send.at[1], deg_recv.at[1], prev),
        remote(deg_sum.at[2], far_deg.at[0], deg_send.at[2], deg_recv.at[2], far_next),
        remote(deg_sum.at[0], far_deg.at[1], deg_send.at[3], deg_recv.at[3], far_prev),
    ]
    for copy in deg_copies:
        copy.start()
    for copy in start_copies + deg_copies:
        copy.wait_recv()
    inv_root = unfolded(lax.rsqrt(deg_sum[1] + near_deg[0, 1] + near_deg[1, 0]))
    inv_prev = unfolded(lax.rsqrt(deg_sum[0] + near_deg[0, 0] + far_deg[0]))
    inv_next = unfolded(lax.rsqrt(deg_sum[2] + near_deg[1, 1] + far_deg[1]))

    pending = deg_copies + start_copies + moving[0] + moving[1]
    sent_only = []

    def product(vectors, tile, c0, c_count):
        return jnp.dot(vectors, tiles[tile, :, pl.ds(c0, c_count)], preferred_element_type=F32)

    def reduce_send(it, phase, packed):
        gram[it, phase] = packed
        copies = []
        for k, device in enumerate(phases[phase]):
            slot = base[phase] + mirror[phase][k]
            copy = remote(
                gram.at[it, phase],
                got_gram.at[it, slot],
                gram_send.at[it, base[phase] + k],
                gram_recv.at[it, slot],
                device,
            )
            copy.start()
            copies.append(copy)
        sent_only.extend(copies)
        return copies

    def reduce_wait(it, phase, packed, copies):
        for copy in copies:
            copy.wait_recv()
        for k in range(len(phases[phase])):
            packed = packed + got_gram[it, base[phase] + k]
        return packed

    def no_beside(stage_index):
        return None

    def scaled_start(side, inverse):
        return (got_x[side].astype(F32) * inverse).astype(BF16)

    def apply_affinity(it, vectors, beside):
        beside(0)
        own_scaled = (vectors * inv_root).astype(BF16)
        copies = []
        if it:
            scaled[it - 1] = own_scaled
            for device, side in both:
                copy = remote(
                    scaled.at[it - 1],
                    got_scaled.at[it - 1, side],
                    vec_send.at[it - 1, side],
                    vec_recv.at[it - 1, side],
                    device,
                )
                copy.start()
                copies.append(copy)
            sent_only.extend(copies)
        total = product(own_scaled, OO, 0, PTS)
        to_prev = product(own_scaled, OP, 0, PTS)
        beside(1)
        if it:
            for copy in copies:
                copy.wait_recv()
            from_prev, from_next = got_scaled[it - 1, 0], got_scaled[it - 1, 1]
        else:
            from_prev, from_next = scaled_start(0, inv_prev), scaled_start(1, inv_next)
        part_copies = []
        for half in range(2):
            at = pl.ds(half * HALF, HALF)
            for device, side in both:
                if side == 0:
                    piece = product(from_prev, PN, half * HALF, HALF)
                else:
                    piece = to_prev[:, half * HALF : (half + 1) * HALF]
                    piece = piece + product(from_next, NP, half * HALF, HALF)
                part[it, side, half] = piece.astype(PARTIAL)
                copy = remote(
                    part.at[it, side, half],
                    got_part.at[it, side, half],
                    part_send.at[it, side, half],
                    part_recv.at[it, side, half],
                    device,
                )
                copy.start()
                part_copies.append(copy)
        sent_only.extend(part_copies)
        total = total + product(from_prev, PO, 0, PTS)
        beside(2)
        for copy in part_copies:
            copy.wait_recv()
        halves = [
            got_part[it, 0, half].astype(F32) + got_part[it, 1, half].astype(F32) for half in range(2)
        ]
        return (total + jnp.concatenate(halves, axis=1)) * inv_root

    scale = math.sqrt(n_row * n_col * PTS)
    image = apply_affinity(0, x_cols[...], no_beside)
    for it in range(1, ITERS):
        state = {}

        def beside(stage_index):
            if stage_index == 0:
                state["sum"] = gram_packed(image)
            else:
                state["sum"] = reduce_wait(it - 1, stage_index - 1, state["sum"], state["copies"])
            if stage_index < len(phases):
                state["copies"] = reduce_send(it - 1, stage_index, state["sum"])
            else:
                factors[it - 1] = inverse_factor(state["sum"]) * scale

        following = apply_affinity(it, image, beside)
        image = apply_factor(factors[it - 1], following)

    packed = gram_packed(image)
    for phase in range(len(phases)):
        copies = reduce_send(ITERS - 1, phase, packed)
        packed = reduce_wait(ITERS - 1, phase, packed, copies)
    result = apply_factor(inverse_factor(packed) * scale, image)
    out[...] = result

    for copy in pending + sent_only:
        copy.wait_send()


def on_device(n_row, n_col, embeddings, neighbour_ids, start_vectors):
    sums = n_row - 1 + n_col - 1
    n_chunks = len(CHUNKS)
    return pl.pallas_call(
        functools.partial(kernel, n_row, n_col),
        out_shape=jax.ShapeDtypeStruct((K, PTS), F32),
        in_specs=[
            pl.BlockSpec(memory_space=pl.ANY),
            pl.BlockSpec(memory_space=pl.ANY),
            pl.BlockSpec(memory_space=pl.ANY),
        ],
        out_specs=pl.BlockSpec(memory_space=pltpu.VMEM),
        scratch_shapes=[
            pltpu.VMEM((PTS, D), F32),
            pltpu.VMEM((3, PTS, D), BF16),
            pltpu.VMEM((5, PTS, PTS), BF16),
            pltpu.VMEM((K, PTS), F32),
            pltpu.VMEM((BLK_DEV, SLOTS), jnp.int32),
            pltpu.VMEM((8, 128), F32),
            pltpu.VMEM((2, 8, 128), F32),
            pltpu.VMEM((16, PTS), F32),
            pltpu.VMEM((3, 8, PTS), F32),
            pltpu.VMEM((3, 8, 128), F32),
            pltpu.VMEM((2, 2, 8, 128), F32),
            pltpu.VMEM((2, 8, 128), F32),
            pltpu.VMEM((K, PTS), BF16),
            pltpu.VMEM((2, K, PTS), BF16),
            pltpu.VMEM((ITERS - 1, K, K), F32),
            pltpu.VMEM((ITERS - 1, K, PTS), BF16),
            pltpu.VMEM((ITERS - 1, 2, K, PTS), BF16),
            pltpu.VMEM((ITERS, 2, 2, K, HALF), PARTIAL),
            pltpu.VMEM((ITERS, 2, 2, K, HALF), PARTIAL),
            pltpu.VMEM((ITERS, 2, K // 2, 2 * K), F32),
            pltpu.VMEM((ITERS, sums, K // 2, 2 * K), F32),
            pltpu.SemaphoreType.DMA((n_chunks,)),
            pltpu.SemaphoreType.DMA((2,)),
            pltpu.SemaphoreType.DMA((2, n_chunks)),
            pltpu.SemaphoreType.DMA((2, n_chunks)),
            pltpu.SemaphoreType.DMA((2,)),
            pltpu.SemaphoreType.DMA((2,)),
            pltpu.SemaphoreType.DMA((4,)),
            pltpu.SemaphoreType.DMA((4,)),
            pltpu.SemaphoreType.DMA((2,)),
            pltpu.SemaphoreType.DMA((2,)),
            pltpu.SemaphoreType.DMA((ITERS - 1, 2)),
            pltpu.SemaphoreType.DMA((ITERS - 1, 2)),
            pltpu.SemaphoreType.DMA((ITERS, 2, 2)),
            pltpu.SemaphoreType.DMA((ITERS, 2, 2)),
            pltpu.SemaphoreType.DMA((ITERS, sums)),
            pltpu.SemaphoreType.DMA((ITERS, sums)),
        ],
        compiler_params=pltpu.CompilerParams(
            collective_id=0, has_side_effects=True, vmem_limit_bytes=63 * 2**20
        ),
    )(embeddings, neighbour_ids, start_vectors.T).T


def solution(mesh):
    split = P(("row", "col"), None)
    return jax.shard_map(
        functools.partial(on_device, mesh.shape["row"], mesh.shape["col"]),
        mesh=mesh,
        in_specs=(split, split, split),
        out_specs=split,
        check_vma=False,
    )
```

```python
import functools
import math

import jax
import jax.numpy as jnp
from jax import lax
from jax.experimental import pallas as pl
from jax.experimental.pallas import tpu as pltpu
from jax.sharding import PartitionSpec as P

D = 1024
BS = 512
SLOTS = 12
K = 64
REACH = 2
ITERS = 3
BLK_DEV = 2
PTS = BS * BLK_DEV
SHARP = 8.0
EPSILON = 1e-06
CORES = 2
Z_CHIPS = 4
MESH = pl.DeviceIdType.MESH
BF16 = jnp.bfloat16
F32 = jnp.float32

CHUNKS = ((0, 256), (256, 256), (512, 256), (768, 256))
SPLIT = ((0, 768), (768, 256))
PARTIAL = BF16
HALF = PTS // 2
OO, PO, OP, NP, PN = range(5)
OWN, PREV, NEXT = range(3)


def split_hi_lo(x):
    hi = x.astype(BF16)
    return hi, (x - hi.astype(F32)).astype(BF16)


def gram_packed(image):
    hi, lo = split_hi_lo(image)
    both = jnp.concatenate([hi, lo], axis=0)
    full = lax.dot_general(both, both, (((1,), (1,)), ((), ())), preferred_element_type=F32)
    top = full[:K] + full[K:]
    gram = top[:, :K] + top[:, K:]
    return jnp.concatenate([gram[: K // 2], gram[K // 2 :]], axis=1)


def inverse_factor(packed):
    gram = jnp.concatenate([packed[:, :K], packed[:, K:]], axis=0)
    row_ids = lax.broadcasted_iota(jnp.int32, (K, K), 0)
    col_ids = lax.broadcasted_iota(jnp.int32, (K, K), 1)
    eye = jnp.where(row_ids == col_ids, 1.0, 0.0).astype(F32)
    work = jnp.concatenate([gram, eye], axis=1)
    in_group = lax.broadcasted_iota(jnp.int32, (8, 2 * K), 0)
    groups = [work[8 * g : 8 * g + 8] for g in range(K // 8)]

    def wide(value):
        return jnp.broadcast_to(value, (8, 2 * K))

    for k in range(0, K, 4):
        first, r = divmod(k, 8)
        head = groups[first]
        rows = [wide(head[r + i : r + i + 1]) for i in range(4)]
        p = {
            (i, j): wide(head[r + i : r + i + 1, k + j : k + j + 1])
            for i in range(4)
            for j in range(i, 4)
        }
        columns = [[wide(group[:, k + i : k + i + 1]) for i in range(4)] for group in groups[first:]]
        a, b, d = p[0, 0], p[0, 1], p[1, 1]
        inv_a = 1.0 / a
        inv_det = 1.0 / (a * d - b * b)
        d_, b_, a_ = d * inv_det, b * inv_det, a * inv_det
        w = {j: (d_ * p[0, j] - b_ * p[1, j], a_ * p[1, j] - b_ * p[0, j]) for j in (2, 3)}
        u0 = d_ * rows[0] - b_ * rows[1]
        u1 = a_ * rows[1] - b_ * rows[0]
        s22 = p[2, 2] - w[2][0] * p[0, 2] - w[2][1] * p[1, 2]
        s23 = p[2, 3] - w[2][0] * p[0, 3] - w[2][1] * p[1, 3]
        s33 = p[3, 3] - w[3][0] * p[0, 3] - w[3][1] * p[1, 3]
        inv_s22 = 1.0 / s22
        inv_rest = 1.0 / (s22 * s33 - s23 * s23)
        s2 = rows[2] - p[0, 2] * u0 - p[1, 2] * u1
        s3 = rows[3] - p[0, 3] * u0 - p[1, 3] * u1
        t2 = (s33 * inv_rest) * s2 - (s23 * inv_rest) * s3
        t3 = (s22 * inv_rest) * s3 - (s23 * inv_rest) * s2
        t0 = u0 - w[2][0] * t2 - w[3][0] * t3
        t1 = u1 - w[2][1] * t2 - w[3][1] * t3
        for g in range(first, K // 8):
            c = columns[g - first]
            below = groups[g]
            new = below - (c[0] * t0 + c[1] * t1) - (c[2] * t2 + c[3] * t3)
            if g == first:
                second = rows[1] - (b * inv_a) * rows[0]
                fourth = s3 - (s23 * inv_s22) * s2
                kept = jnp.where(in_group == r + 2, s2, jnp.where(in_group == r + 3, fourth, below))
                kept = jnp.where(in_group == r + 1, second, kept)
                new = jnp.where(in_group > r + 3, new, kept)
            groups[g] = new
    work = jnp.concatenate(groups, axis=0)
    pivots = jnp.sum(work[:, :K] * eye, axis=1, keepdims=True)
    return work[:, K:] * lax.rsqrt(pivots)


def folded(row):
    return jnp.concatenate([row[:, 128 * g : 128 * g + 128] for g in range(PTS // 128)], axis=0)


def unfolded(tile):
    return jnp.concatenate([tile[g : g + 1] for g in range(PTS // 128)], axis=1)


def apply_factor(inverse, image):
    mh, ml = split_hi_lo(inverse)
    zh, zl = split_hi_lo(image)
    left = jnp.concatenate([mh, mh, ml, ml], axis=1)
    right = jnp.concatenate([zh, zl, zh, zl], axis=0)
    return jnp.dot(left, right, preferred_element_type=F32)


def kernel(
    n_row, n_col,
    emb, ids_given, start, out,
    stage, normed, tiles, x_cols, ids, own_mask, got_mask, masks, deg, deg_sum, near_deg, far_deg,
    x_half, got_x, factors, wide, tall, whole_gram,
    scaled, got_scaled, part, got_part, gram, half_gram, got_gram,
    load_sem, x_sem, emb_send, emb_recv, mask_send, mask_recv, deg_send, deg_recv, start_send, start_recv,
    vec_send, vec_recv, part_send, part_recv, gram_send, gram_recv,
):
    row, col = lax.axis_index("row"), lax.axis_index("col")
    prev = (row, lax.rem(col + n_col - 1, n_col))
    nxt = (row, lax.rem(col + 1, n_col))
    n_y, n_x = n_row // CORES, n_col // Z_CHIPS
    y, core = row // CORES, lax.rem(row, CORES)
    x, z = col // Z_CHIPS, lax.rem(col, Z_CHIPS)
    def farthest_first(n_a, n_b):
        pairs = [(a, b) for a in range(n_a) for b in range(n_b) if a or b]
        return sorted(pairs, key=lambda s: -min(s[0], n_a - s[0]) - min(s[1], n_b - s[1]))

    steps = [farthest_first(n_y, CORES), farthest_first(n_x, Z_CHIPS), [(0, 1)]]
    other_core = (y * CORES + (1 - core), col)
    phases = [
        [(lax.rem(y + a, n_y) * CORES + lax.rem(core + b, CORES), col) for a, b in steps[0]],
        [(row, lax.rem(x + a, n_x) * Z_CHIPS + lax.rem(z + b, Z_CHIPS)) for a, b in steps[1]],
    ]
    mirror = [
        [steps[0].index((-a % n_y, -b % CORES)) for a, b in steps[0]],
        [steps[1].index((-a % n_x, -b % Z_CHIPS)) for a, b in steps[1]],
    ]
    base = [0, len(steps[0]), len(steps[0]) + len(steps[1])]
    part_rows = K // 2 // CORES

    def rows_of(which):
        return pl.ds(pl.multiple_of(which * part_rows, part_rows), part_rows)

    loads = []
    for i, (begin, count) in enumerate(CHUNKS):
        load = pltpu.make_async_copy(
            emb.at[pl.ds(begin, count)], stage.at[pl.ds(begin, count)], load_sem.at[i]
        )
        load.start()
        loads.append(load)
    x_load = pltpu.make_async_copy(start, x_cols, x_sem.at[0])
    x_load.start()
    ids_load = pltpu.make_async_copy(ids_given, ids, x_sem.at[1])
    ids_load.start()

    barrier = pltpu.get_barrier_semaphore()
    friends = [d for p in phases for d in p]
    for friend in friends:
        pl.semaphore_signal(barrier, inc=1, device_id=friend, device_id_type=MESH)

    lane = lax.broadcasted_iota(jnp.int32, (BLK_DEV, 128), 1)
    holder = col + (lane >> 1) - REACH
    holder = jnp.where(holder < 0, holder + n_col, jnp.where(holder >= n_col, holder - n_col, holder))
    target = (row * n_col + holder) * BLK_DEV + (lane & 1)
    me = (row * n_col + col) * BLK_DEV + lax.broadcasted_iota(jnp.int32, (BLK_DEV, 128), 0)
    ids_load.wait()
    count_listed = jnp.zeros((BLK_DEV, 128), F32)
    for slot in range(SLOTS):
        named = ids[:, slot : slot + 1]
        hit = named == target
        if slot:
            hit = hit & (named != me)
        count_listed += jnp.where(hit, 1.0, 0.0)
    own_mask[...] = jnp.zeros((8, 128), F32)
    own_mask[0:BLK_DEV, :] = count_listed

    def normalize(begin, count):
        step = 32

        def some(i, carry):
            rows = pl.ds(begin + i * step, step)
            e = stage[rows, :]
            inv = lax.rsqrt(jnp.mean(e * e, axis=-1, keepdims=True) + EPSILON)
            normed[OWN, rows, :] = (e * inv).astype(BF16)
            return carry

        lax.fori_loop(0, count // step, some, 0)

    def remote(src, dst, send, recv, device):
        return pltpu.make_async_remote_copy(
            src_ref=src, dst_ref=dst, send_sem=send, recv_sem=recv, device_id=device, device_id_type=MESH
        )

    both = ((nxt, 0), (prev, 1))
    moving = [[], []]
    start_copies = []
    mask_copies = []
    for i, (begin, count) in enumerate(CHUNKS):
        loads[i].wait()
        normalize(begin, count)
        if i == 0:
            pl.semaphore_wait(barrier, len(friends))
            for device, side in both:
                copy = remote(own_mask, got_mask.at[side], mask_send.at[side], mask_recv.at[side], device)
                copy.start()
                mask_copies.append(copy)
        rows = pl.ds(begin, count)
        for first, width in SPLIT if i == len(CHUNKS) - 1 else ((0, D),):
            for device, side in both:
                at = len(moving[side])
                copy = remote(
                    normed.at[OWN, rows, pl.ds(first, width)],
                    normed.at[PREV + side, rows, pl.ds(first, width)],
                    emb_send.at[side, at],
                    emb_recv.at[side, at],
                    device,
                )
                copy.start()
                moving[side].append(copy)
        if i == 0:
            x_load.wait()
            x_half[...] = x_cols[...].astype(BF16)
            for device, side in both:
                copy = remote(x_half, got_x.at[side], start_send.at[side], start_recv.at[side], device)
                copy.start()
                start_copies.append(copy)

    first_block = lax.broadcasted_iota(jnp.int32, (1, PTS), 1) < BS

    def spread_mask(tile, listing, candidate):
        for block in range(BLK_DEV):
            at = candidate + block
            masks[pl.ds(2 * tile + block, 1), :] = jnp.where(
                first_block, listing[0:1, at : at + 1], listing[1:2, at : at + 1]
            )

    def offset_at(offset):
        return (offset + REACH) * BLK_DEV

    left = {OO: OWN, PO: PREV, OP: OWN, NP: NEXT, PN: PREV}
    right = {OO: OWN, PO: OWN, OP: PREV, NP: PREV, PN: NEXT}

    def dots(tile, r0, r_count, c0, c_count, first=0, width=D):
        a = normed[left[tile], pl.ds(r0, r_count), pl.ds(first, width)]
        b = normed[right[tile], pl.ds(c0, c_count), pl.ds(first, width)]
        return lax.dot_general(a, b, (((1,), (1,)), ((), ())), preferred_element_type=F32)

    def affinity(tile, r0, r_count, c0, c_count, product=None):
        if product is None:
            product = dots(tile, r0, r_count, c0, c_count)
        value = jnp.exp(product * (SHARP / D) - SHARP)
        lists = [masks[pl.ds(2 * tile + block, 1), pl.ds(c0, c_count)] for block in range(BLK_DEV)]
        if r0 < BS < r0 + r_count:
            above = BS - r0
            value = jnp.concatenate([value[:above] * lists[0], value[above:] * lists[1]], axis=0)
        else:
            value = value * lists[r0 // BS]
        tiles[tile, pl.ds(r0, r_count), pl.ds(c0, c_count)] = value.astype(BF16)
        deg[right[tile], :, pl.ds(c0, c_count)] += jnp.sum(
            value.reshape(r_count // 8, 8, c_count), axis=0
        )

    deg[...] = jnp.zeros((3, 8, PTS), F32)
    mine = own_mask[...]
    spread_mask(OO, mine, offset_at(0))
    spread_mask(PO, mine, offset_at(-1))
    for begin, count in CHUNKS:
        affinity(OO, begin, count, 0, PTS)
    for copy in mask_copies:
        copy.wait()
    theirs = got_mask[0]
    spread_mask(OP, theirs, offset_at(1))
    spread_mask(NP, theirs, offset_at(2))
    spread_mask(PN, got_mask[1], offset_at(-2))

    for i, (begin, count) in enumerate(CHUNKS[:-1]):
        moving[0][i].wait_recv()
        affinity(PO, begin, count, 0, PTS)
        affinity(OP, 0, PTS, begin, count)
        moving[1][i].wait_recv()
        end = begin + count
        affinity(NP, begin, count, 0, end)
        affinity(PN, begin, count, 0, end)
        if begin:
            affinity(NP, 0, begin, begin, count)
            affinity(PN, 0, begin, begin, count)

    begin, count = CHUNKS[-1]
    last = len(CHUNKS) - 1
    blocks = (
        (PO, begin, count, 0, PTS, wide.at[0]),
        (OP, 0, PTS, begin, count, tall.at[0]),
        (NP, begin, count, 0, PTS, wide.at[1]),
        (PN, begin, count, 0, PTS, wide.at[2]),
        (NP, 0, begin, begin, count, tall.at[1, pl.ds(0, begin)]),
        (PN, 0, begin, begin, count, tall.at[2, pl.ds(0, begin)]),
    )
    for part_index, (first, width) in enumerate(SPLIT):
        moving[0][last + part_index].wait_recv()
        moving[1][last + part_index].wait_recv()
        for tile, r0, r_count, c0, c_count, kept in blocks:
            if part_index == 0:
                kept[...] = dots(tile, r0, r_count, c0, c_count, first, width)
            else:
                total = kept[...] + dots(tile, r0, r_count, c0, c_count, first, width)
                affinity(tile, r0, r_count, c0, c_count, total)

    for place, where in enumerate((PREV, OWN, NEXT)):
        deg_sum[place] = folded(jnp.sum(deg[where], axis=0, keepdims=True))
    far_prev = (row, lax.rem(col + n_col - 2, n_col))
    far_next = (row, lax.rem(col + 2, n_col))
    deg_copies = [
        remote(deg_sum.at[pl.ds(1, 2)], near_deg.at[0], deg_send.at[0], deg_recv.at[0], nxt),
        remote(deg_sum.at[pl.ds(0, 2)], near_deg.at[1], deg_send.at[1], deg_recv.at[1], prev),
        remote(deg_sum.at[2], far_deg.at[0], deg_send.at[2], deg_recv.at[2], far_next),
        remote(deg_sum.at[0], far_deg.at[1], deg_send.at[3], deg_recv.at[3], far_prev),
    ]
    for copy in deg_copies:
        copy.start()
    for copy in start_copies + deg_copies:
        copy.wait_recv()
    inv_root = unfolded(lax.rsqrt(deg_sum[1] + near_deg[0, 1] + near_deg[1, 0]))
    inv_prev = unfolded(lax.rsqrt(deg_sum[0] + near_deg[0, 0] + far_deg[0]))
    inv_next = unfolded(lax.rsqrt(deg_sum[2] + near_deg[1, 1] + far_deg[1]))

    pending = deg_copies + start_copies + moving[0] + moving[1]
    sent_only = []

    def product(vectors, tile, c0, c_count):
        return jnp.dot(vectors, tiles[tile, :, pl.ds(c0, c_count)], preferred_element_type=F32)

    def reduce_send(it, phase, packed):
        copies = []
        if phase == 0:
            gram[it] = packed
            for k, device in enumerate(phases[0]):
                theirs = lax.rem(core + steps[0][k][1], CORES)
                copies.append((gram.at[it, rows_of(theirs)], got_gram, mirror[0][k], k, device))
        elif phase == 1:
            half_gram[it] = packed
            for k, device in enumerate(phases[1]):
                slot = base[1] + mirror[1][k]
                copies.append((half_gram.at[it], got_gram, slot, base[1] + k, device))
        else:
            whole_gram[it, rows_of(core), :] = packed
            mine = whole_gram.at[it, rows_of(core)]
            copies.append((mine, None, base[2], base[2], other_core))
        started = []
        for src, landing, slot, k, device in copies:
            dst = src if landing is None else landing.at[it, slot]
            copy = remote(src, dst, gram_send.at[it, k], gram_recv.at[it, slot], device)
            copy.start()
            started.append(copy)
        sent_only.extend(started)
        return started

    def reduce_wait(it, phase, packed, copies):
        for copy in copies:
            copy.wait_recv()
        if phase == 2:
            return whole_gram[it]
        if phase == 0:
            packed = gram[it, rows_of(core), :]
        for k in range(len(phases[phase])):
            packed = packed + got_gram[it, base[phase] + k]
        return packed

    def no_beside(stage_index):
        return None

    def scaled_start(side, inverse):
        return (got_x[side].astype(F32) * inverse).astype(BF16)

    def apply_affinity(it, vectors, beside):
        beside(0)
        own_scaled = (vectors * inv_root).astype(BF16)
        copies = []
        if it:
            scaled[it - 1] = own_scaled
            for device, side in both:
                copy = remote(
                    scaled.at[it - 1],
                    got_scaled.at[it - 1, side],
                    vec_send.at[it - 1, side],
                    vec_recv.at[it - 1, side],
                    device,
                )
                copy.start()
                copies.append(copy)
            sent_only.extend(copies)
        total = product(own_scaled, OO, 0, PTS)
        to_prev = product(own_scaled, OP, 0, PTS)
        beside(1)
        if it:
            for copy in copies:
                copy.wait_recv()
            from_prev, from_next = got_scaled[it - 1, 0], got_scaled[it - 1, 1]
        else:
            from_prev, from_next = scaled_start(0, inv_prev), scaled_start(1, inv_next)
        part_copies = []
        for half in range(2):
            at = pl.ds(half * HALF, HALF)
            for device, side in both:
                if side == 0:
                    piece = product(from_prev, PN, half * HALF, HALF)
                else:
                    piece = to_prev[:, half * HALF : (half + 1) * HALF]
                    piece = piece + product(from_next, NP, half * HALF, HALF)
                part[it, side, half] = piece.astype(PARTIAL)
                copy = remote(
                    part.at[it, side, half],
                    got_part.at[it, side, half],
                    part_send.at[it, side, half],
                    part_recv.at[it, side, half],
                    device,
                )
                copy.start()
                part_copies.append(copy)
        sent_only.extend(part_copies)
        total = total + product(from_prev, PO, 0, PTS)
        beside(2)
        beside(3)
        for copy in part_copies:
            copy.wait_recv()
        halves = [
            got_part[it, 0, half].astype(F32) + got_part[it, 1, half].astype(F32) for half in range(2)
        ]
        return (total + jnp.concatenate(halves, axis=1)) * inv_root

    scale = math.sqrt(n_row * n_col * PTS)
    image = apply_affinity(0, x_cols[...], no_beside)
    for it in range(1, ITERS):
        state = {}

        def beside(stage_index):
            if stage_index == 0:
                state["sum"] = gram_packed(image)
            else:
                state["sum"] = reduce_wait(it - 1, stage_index - 1, state["sum"], state["copies"])
            if stage_index < 3:
                state["copies"] = reduce_send(it - 1, stage_index, state["sum"])
            else:
                factors[it - 1] = inverse_factor(state["sum"]) * scale

        following = apply_affinity(it, image, beside)
        image = apply_factor(factors[it - 1], following)

    packed = gram_packed(image)
    for phase in range(3):
        copies = reduce_send(ITERS - 1, phase, packed)
        packed = reduce_wait(ITERS - 1, phase, packed, copies)
    result = apply_factor(inverse_factor(packed) * scale, image)
    out[...] = result

    for copy in pending + sent_only:
        copy.wait_send()


def on_device(n_row, n_col, embeddings, neighbour_ids, start_vectors):
    sums = n_row - 1 + n_col - 1 + 1
    n_chunks = len(CHUNKS) + len(SPLIT) - 1
    return pl.pallas_call(
        functools.partial(kernel, n_row, n_col),
        out_shape=jax.ShapeDtypeStruct((K, PTS), F32),
        in_specs=[
            pl.BlockSpec(memory_space=pl.ANY),
            pl.BlockSpec(memory_space=pl.ANY),
            pl.BlockSpec(memory_space=pl.ANY),
        ],
        out_specs=pl.BlockSpec(memory_space=pltpu.VMEM),
        scratch_shapes=[
            pltpu.VMEM((PTS, D), F32),
            pltpu.VMEM((3, PTS, D), BF16),
            pltpu.VMEM((5, PTS, PTS), BF16),
            pltpu.VMEM((K, PTS), F32),
            pltpu.VMEM((BLK_DEV, SLOTS), jnp.int32),
            pltpu.VMEM((8, 128), F32),
            pltpu.VMEM((2, 8, 128), F32),
            pltpu.VMEM((16, PTS), F32),
            pltpu.VMEM((3, 8, PTS), F32),
            pltpu.VMEM((3, 8, 128), F32),
            pltpu.VMEM((2, 2, 8, 128), F32),
            pltpu.VMEM((2, 8, 128), F32),
            pltpu.VMEM((K, PTS), BF16),
            pltpu.VMEM((2, K, PTS), BF16),
            pltpu.VMEM((ITERS - 1, K, K), F32),
            pltpu.VMEM((3, CHUNKS[-1][1], PTS), F32),
            pltpu.VMEM((3, PTS, CHUNKS[-1][1]), F32),
            pltpu.VMEM((ITERS, K // 2, 2 * K), F32),
            pltpu.VMEM((ITERS - 1, K, PTS), BF16),
            pltpu.VMEM((ITERS - 1, 2, K, PTS), BF16),
            pltpu.VMEM((ITERS, 2, 2, K, HALF), PARTIAL),
            pltpu.VMEM((ITERS, 2, 2, K, HALF), PARTIAL),
            pltpu.VMEM((ITERS, K // 2, 2 * K), F32),
            pltpu.VMEM((ITERS, K // 2 // CORES, 2 * K), F32),
            pltpu.VMEM((ITERS, sums, K // 2 // CORES, 2 * K), F32),
            pltpu.SemaphoreType.DMA((n_chunks,)),
            pltpu.SemaphoreType.DMA((2,)),
            pltpu.SemaphoreType.DMA((2, n_chunks)),
            pltpu.SemaphoreType.DMA((2, n_chunks)),
            pltpu.SemaphoreType.DMA((2,)),
            pltpu.SemaphoreType.DMA((2,)),
            pltpu.SemaphoreType.DMA((4,)),
            pltpu.SemaphoreType.DMA((4,)),
            pltpu.SemaphoreType.DMA((2,)),
            pltpu.SemaphoreType.DMA((2,)),
            pltpu.SemaphoreType.DMA((ITERS - 1, 2)),
            pltpu.SemaphoreType.DMA((ITERS - 1, 2)),
            pltpu.SemaphoreType.DMA((ITERS, 2, 2)),
            pltpu.SemaphoreType.DMA((ITERS, 2, 2)),
            pltpu.SemaphoreType.DMA((ITERS, sums)),
            pltpu.SemaphoreType.DMA((ITERS, sums)),
        ],
        compiler_params=pltpu.CompilerParams(
            collective_id=0, has_side_effects=True, vmem_limit_bytes=63 * 2**20
        ),
    )(embeddings, neighbour_ids, start_vectors.T).T


def solution(mesh):
    split = P(("row", "col"), None)
    return jax.shard_map(
        functools.partial(on_device, mesh.shape["row"], mesh.shape["col"]),
        mesh=mesh,
        in_specs=(split, split, split),
        out_specs=split,
        check_vma=False,
    )
```

```python
import functools
import math

import jax
import jax.numpy as jnp
from jax import lax
from jax.experimental import pallas as pl
from jax.experimental.pallas import tpu as pltpu
from jax.sharding import PartitionSpec as P

D = 1024
BS = 512
SLOTS = 12
K = 64
REACH = 2
ITERS = 3
BLK_DEV = 2
PTS = BS * BLK_DEV
SHARP = 8.0
EPSILON = 1e-06
CORES = 2
Z_CHIPS = 4
MESH = pl.DeviceIdType.MESH
BF16 = jnp.bfloat16
F32 = jnp.float32

CHUNKS = ((0, 256), (256, 256), (512, 256), (768, 256))
SPLIT = ((0, 768), (768, 256))
PARTIAL = BF16
HALF = PTS // 2
OO, PO, OP, NP, PN = range(5)
OWN, PREV, NEXT = range(3)


def split_hi_lo(x):
    hi = x.astype(BF16)
    return hi, (x - hi.astype(F32)).astype(BF16)


def gram_packed(image):
    hi, lo = split_hi_lo(image)
    both = jnp.concatenate([hi, lo], axis=0)
    full = lax.dot_general(both, both, (((1,), (1,)), ((), ())), preferred_element_type=F32)
    top = full[:K] + full[K:]
    gram = top[:, :K] + top[:, K:]
    return jnp.concatenate([gram[: K // 2], gram[K // 2 :]], axis=1)


def inverse_factor(packed):
    gram = jnp.concatenate([packed[:, :K], packed[:, K:]], axis=0)
    row_ids = lax.broadcasted_iota(jnp.int32, (K, K), 0)
    col_ids = lax.broadcasted_iota(jnp.int32, (K, K), 1)
    eye = jnp.where(row_ids == col_ids, 1.0, 0.0).astype(F32)
    work = jnp.concatenate([gram, eye], axis=1)
    in_group = lax.broadcasted_iota(jnp.int32, (8, 2 * K), 0)
    groups = [work[8 * g : 8 * g + 8] for g in range(K // 8)]

    def wide(value):
        return jnp.broadcast_to(value, (8, 2 * K))

    for k in range(0, K, 4):
        first, r = divmod(k, 8)
        head = groups[first]
        rows = [wide(head[r + i : r + i + 1]) for i in range(4)]
        p = {
            (i, j): wide(head[r + i : r + i + 1, k + j : k + j + 1])
            for i in range(4)
            for j in range(i, 4)
        }
        columns = [[wide(group[:, k + i : k + i + 1]) for i in range(4)] for group in groups[first:]]
        a, b, d = p[0, 0], p[0, 1], p[1, 1]
        inv_a = 1.0 / a
        inv_det = 1.0 / (a * d - b * b)
        d_, b_, a_ = d * inv_det, b * inv_det, a * inv_det
        w = {j: (d_ * p[0, j] - b_ * p[1, j], a_ * p[1, j] - b_ * p[0, j]) for j in (2, 3)}
        u0 = d_ * rows[0] - b_ * rows[1]
        u1 = a_ * rows[1] - b_ * rows[0]
        s22 = p[2, 2] - w[2][0] * p[0, 2] - w[2][1] * p[1, 2]
        s23 = p[2, 3] - w[2][0] * p[0, 3] - w[2][1] * p[1, 3]
        s33 = p[3, 3] - w[3][0] * p[0, 3] - w[3][1] * p[1, 3]
        inv_s22 = 1.0 / s22
        inv_rest = 1.0 / (s22 * s33 - s23 * s23)
        s2 = rows[2] - p[0, 2] * u0 - p[1, 2] * u1
        s3 = rows[3] - p[0, 3] * u0 - p[1, 3] * u1
        t2 = (s33 * inv_rest) * s2 - (s23 * inv_rest) * s3
        t3 = (s22 * inv_rest) * s3 - (s23 * inv_rest) * s2
        t0 = u0 - w[2][0] * t2 - w[3][0] * t3
        t1 = u1 - w[2][1] * t2 - w[3][1] * t3
        for g in range(first, K // 8):
            c = columns[g - first]
            below = groups[g]
            new = below - (c[0] * t0 + c[1] * t1) - (c[2] * t2 + c[3] * t3)
            if g == first:
                second = rows[1] - (b * inv_a) * rows[0]
                fourth = s3 - (s23 * inv_s22) * s2
                kept = jnp.where(in_group == r + 2, s2, jnp.where(in_group == r + 3, fourth, below))
                kept = jnp.where(in_group == r + 1, second, kept)
                new = jnp.where(in_group > r + 3, new, kept)
            groups[g] = new
    work = jnp.concatenate(groups, axis=0)
    pivots = jnp.sum(work[:, :K] * eye, axis=1, keepdims=True)
    return work[:, K:] * lax.rsqrt(pivots)


def folded(row):
    return jnp.concatenate([row[:, 128 * g : 128 * g + 128] for g in range(PTS // 128)], axis=0)


def unfolded(tile):
    return jnp.concatenate([tile[g : g + 1] for g in range(PTS // 128)], axis=1)


def apply_factor(inverse, image):
    mh, ml = split_hi_lo(inverse)
    zh, zl = split_hi_lo(image)
    left = jnp.concatenate([mh, mh, ml, ml], axis=1)
    right = jnp.concatenate([zh, zl, zh, zl], axis=0)
    return jnp.dot(left, right, preferred_element_type=F32)


def kernel(
    n_row, n_col,
    emb, ids_given, start, out,
    stage, normed, tiles, x_cols, ids, own_mask, got_mask, masks, deg, deg_sum, near_deg, far_deg,
    x_half, got_x, factors, wide, tall, whole_gram,
    scaled, got_scaled, part, got_part, gram, half_gram, got_gram,
    load_sem, x_sem, emb_send, emb_recv, mask_send, mask_recv, deg_send, deg_recv, start_send, start_recv,
    vec_send, vec_recv, part_send, part_recv, gram_send, gram_recv,
):
    row, col = lax.axis_index("row"), lax.axis_index("col")
    prev = (row, lax.rem(col + n_col - 1, n_col))
    nxt = (row, lax.rem(col + 1, n_col))
    n_y, n_x = n_row // CORES, n_col // Z_CHIPS
    y, core = row // CORES, lax.rem(row, CORES)
    x, z = col // Z_CHIPS, lax.rem(col, Z_CHIPS)
    def farthest_first(n_a, n_b):
        pairs = [(a, b) for a in range(n_a) for b in range(n_b) if a or b]
        return sorted(pairs, key=lambda s: -min(s[0], n_a - s[0]) - min(s[1], n_b - s[1]))

    steps = [farthest_first(n_y, CORES), farthest_first(n_x, Z_CHIPS), [(0, 1)]]
    other_core = (y * CORES + (1 - core), col)
    phases = [
        [(lax.rem(y + a, n_y) * CORES + lax.rem(core + b, CORES), col) for a, b in steps[0]],
        [(row, lax.rem(x + a, n_x) * Z_CHIPS + lax.rem(z + b, Z_CHIPS)) for a, b in steps[1]],
    ]
    mirror = [
        [steps[0].index((-a % n_y, -b % CORES)) for a, b in steps[0]],
        [steps[1].index((-a % n_x, -b % Z_CHIPS)) for a, b in steps[1]],
    ]
    base = [0, len(steps[0]), len(steps[0]) + len(steps[1])]
    part_rows = K // 2 // CORES

    def rows_of(which):
        return pl.ds(pl.multiple_of(which * part_rows, part_rows), part_rows)

    loads = []
    for i, (begin, count) in enumerate(CHUNKS):
        load = pltpu.make_async_copy(
            emb.at[pl.ds(begin, count)], stage.at[pl.ds(begin, count)], load_sem.at[i]
        )
        load.start()
        loads.append(load)
    x_load = pltpu.make_async_copy(start, x_cols, x_sem.at[0])
    x_load.start()
    ids_load = pltpu.make_async_copy(ids_given, ids, x_sem.at[1])
    ids_load.start()

    barrier = pltpu.get_barrier_semaphore()
    friends = [d for p in phases for d in p]
    for friend in friends:
        pl.semaphore_signal(barrier, inc=1, device_id=friend, device_id_type=MESH)

    lane = lax.broadcasted_iota(jnp.int32, (BLK_DEV, 128), 1)
    holder = col + (lane >> 1) - REACH
    holder = jnp.where(holder < 0, holder + n_col, jnp.where(holder >= n_col, holder - n_col, holder))
    target = (row * n_col + holder) * BLK_DEV + (lane & 1)
    me = (row * n_col + col) * BLK_DEV + lax.broadcasted_iota(jnp.int32, (BLK_DEV, 128), 0)
    ids_load.wait()
    count_listed = jnp.zeros((BLK_DEV, 128), F32)
    for slot in range(SLOTS):
        named = ids[:, slot : slot + 1]
        hit = named == target
        if slot:
            hit = hit & (named != me)
        count_listed += jnp.where(hit, 1.0, 0.0)
    own_mask[...] = jnp.zeros((8, 128), F32)
    own_mask[0:BLK_DEV, :] = count_listed

    def normalize(begin, count):
        step = 32

        def some(i, carry):
            rows = pl.ds(begin + i * step, step)
            e = stage[rows, :]
            inv = lax.rsqrt(jnp.mean(e * e, axis=-1, keepdims=True) + EPSILON)
            normed[OWN, rows, :] = (e * inv).astype(BF16)
            return carry

        lax.fori_loop(0, count // step, some, 0)

    def remote(src, dst, send, recv, device):
        return pltpu.make_async_remote_copy(
            src_ref=src, dst_ref=dst, send_sem=send, recv_sem=recv, device_id=device, device_id_type=MESH
        )

    both = ((nxt, 0), (prev, 1))
    moving = [[], []]
    start_copies = []
    mask_copies = []
    for i, (begin, count) in enumerate(CHUNKS):
        loads[i].wait()
        normalize(begin, count)
        if i == 0:
            pl.semaphore_wait(barrier, len(friends))
            for device, side in both:
                copy = remote(own_mask, got_mask.at[side], mask_send.at[side], mask_recv.at[side], device)
                copy.start()
                mask_copies.append(copy)
        rows = pl.ds(begin, count)
        for first, width in SPLIT if i == len(CHUNKS) - 1 else ((0, D),):
            for device, side in both:
                at = len(moving[side])
                copy = remote(
                    normed.at[OWN, rows, pl.ds(first, width)],
                    normed.at[PREV + side, rows, pl.ds(first, width)],
                    emb_send.at[side, at],
                    emb_recv.at[side, at],
                    device,
                )
                copy.start()
                moving[side].append(copy)
    x_load.wait()
    x_half[...] = x_cols[...].astype(BF16)
    for device, side in both:
        copy = remote(x_half, got_x.at[side], start_send.at[side], start_recv.at[side], device)
        copy.start()
        start_copies.append(copy)

    first_block = lax.broadcasted_iota(jnp.int32, (1, PTS), 1) < BS

    def spread_mask(tile, listing, candidate):
        for block in range(BLK_DEV):
            at = candidate + block
            masks[pl.ds(2 * tile + block, 1), :] = jnp.where(
                first_block, listing[0:1, at : at + 1], listing[1:2, at : at + 1]
            )

    def offset_at(offset):
        return (offset + REACH) * BLK_DEV

    left = {OO: OWN, PO: PREV, OP: OWN, NP: NEXT, PN: PREV}
    right = {OO: OWN, PO: OWN, OP: PREV, NP: PREV, PN: NEXT}

    def dots(tile, r0, r_count, c0, c_count, first=0, width=D):
        a = normed[left[tile], pl.ds(r0, r_count), pl.ds(first, width)]
        b = normed[right[tile], pl.ds(c0, c_count), pl.ds(first, width)]
        return lax.dot_general(a, b, (((1,), (1,)), ((), ())), preferred_element_type=F32)

    def affinity(tile, r0, r_count, c0, c_count, product=None):
        if product is None:
            product = dots(tile, r0, r_count, c0, c_count)
        value = jnp.exp(product * (SHARP / D) - SHARP)
        lists = [masks[pl.ds(2 * tile + block, 1), pl.ds(c0, c_count)] for block in range(BLK_DEV)]
        if r0 < BS < r0 + r_count:
            above = BS - r0
            value = jnp.concatenate([value[:above] * lists[0], value[above:] * lists[1]], axis=0)
        else:
            value = value * lists[r0 // BS]
        tiles[tile, pl.ds(r0, r_count), pl.ds(c0, c_count)] = value.astype(BF16)
        deg[right[tile], :, pl.ds(c0, c_count)] += jnp.sum(
            value.reshape(r_count // 8, 8, c_count), axis=0
        )

    deg[...] = jnp.zeros((3, 8, PTS), F32)
    mine = own_mask[...]
    spread_mask(OO, mine, offset_at(0))
    spread_mask(PO, mine, offset_at(-1))
    for begin, count in CHUNKS:
        affinity(OO, begin, count, 0, PTS)
    for copy in mask_copies:
        copy.wait()
    theirs = got_mask[0]
    spread_mask(OP, theirs, offset_at(1))
    spread_mask(NP, theirs, offset_at(2))
    spread_mask(PN, got_mask[1], offset_at(-2))

    for i, (begin, count) in enumerate(CHUNKS[:-1]):
        moving[0][i].wait_recv()
        affinity(PO, begin, count, 0, PTS)
        affinity(OP, 0, PTS, begin, count)
        moving[1][i].wait_recv()
        end = begin + count
        affinity(NP, begin, count, 0, end)
        affinity(PN, begin, count, 0, end)
        if begin:
            affinity(NP, 0, begin, begin, count)
            affinity(PN, 0, begin, begin, count)

    begin, count = CHUNKS[-1]
    last = len(CHUNKS) - 1
    blocks = (
        (PO, begin, count, 0, PTS, wide.at[0]),
        (OP, 0, PTS, begin, count, tall.at[0]),
        (NP, begin, count, 0, PTS, wide.at[1]),
        (PN, begin, count, 0, PTS, wide.at[2]),
        (NP, 0, begin, begin, count, tall.at[1, pl.ds(0, begin)]),
        (PN, 0, begin, begin, count, tall.at[2, pl.ds(0, begin)]),
    )
    for part_index, (first, width) in enumerate(SPLIT):
        moving[0][last + part_index].wait_recv()
        moving[1][last + part_index].wait_recv()
        for tile, r0, r_count, c0, c_count, kept in blocks:
            if part_index == 0:
                kept[...] = dots(tile, r0, r_count, c0, c_count, first, width)
            else:
                total = kept[...] + dots(tile, r0, r_count, c0, c_count, first, width)
                affinity(tile, r0, r_count, c0, c_count, total)

    for place, where in enumerate((PREV, OWN, NEXT)):
        deg_sum[place] = folded(jnp.sum(deg[where], axis=0, keepdims=True))
    far_prev = (row, lax.rem(col + n_col - 2, n_col))
    far_next = (row, lax.rem(col + 2, n_col))
    deg_copies = [
        remote(deg_sum.at[pl.ds(1, 2)], near_deg.at[0], deg_send.at[0], deg_recv.at[0], nxt),
        remote(deg_sum.at[pl.ds(0, 2)], near_deg.at[1], deg_send.at[1], deg_recv.at[1], prev),
        remote(deg_sum.at[2], far_deg.at[0], deg_send.at[2], deg_recv.at[2], far_next),
        remote(deg_sum.at[0], far_deg.at[1], deg_send.at[3], deg_recv.at[3], far_prev),
    ]
    for copy in deg_copies:
        copy.start()
    for copy in start_copies + deg_copies:
        copy.wait_recv()
    inv_root = unfolded(lax.rsqrt(deg_sum[1] + near_deg[0, 1] + near_deg[1, 0]))
    inv_prev = unfolded(lax.rsqrt(deg_sum[0] + near_deg[0, 0] + far_deg[0]))
    inv_next = unfolded(lax.rsqrt(deg_sum[2] + near_deg[1, 1] + far_deg[1]))

    pending = deg_copies + start_copies + moving[0] + moving[1]
    sent_only = []

    def product(vectors, tile, c0, c_count):
        return jnp.dot(vectors, tiles[tile, :, pl.ds(c0, c_count)], preferred_element_type=F32)

    def reduce_send(it, phase, packed):
        copies = []
        if phase == 0:
            gram[it] = packed
            for k, device in enumerate(phases[0]):
                theirs = lax.rem(core + steps[0][k][1], CORES)
                copies.append((gram.at[it, rows_of(theirs)], got_gram, mirror[0][k], k, device))
        elif phase == 1:
            half_gram[it] = packed
            for k, device in enumerate(phases[1]):
                slot = base[1] + mirror[1][k]
                copies.append((half_gram.at[it], got_gram, slot, base[1] + k, device))
        else:
            whole_gram[it, rows_of(core), :] = packed
            mine = whole_gram.at[it, rows_of(core)]
            copies.append((mine, None, base[2], base[2], other_core))
        started = []
        for src, landing, slot, k, device in copies:
            dst = src if landing is None else landing.at[it, slot]
            copy = remote(src, dst, gram_send.at[it, k], gram_recv.at[it, slot], device)
            copy.start()
            started.append(copy)
        sent_only.extend(started)
        return started

    def reduce_wait(it, phase, packed, copies):
        for copy in copies:
            copy.wait_recv()
        if phase == 2:
            return whole_gram[it]
        if phase == 0:
            packed = gram[it, rows_of(core), :]
        for k in range(len(phases[phase])):
            packed = packed + got_gram[it, base[phase] + k]
        return packed

    def no_beside(stage_index):
        return None

    def scaled_start(side, inverse):
        return (got_x[side].astype(F32) * inverse).astype(BF16)

    def apply_affinity(it, vectors, beside):
        own_scaled = (vectors * inv_root).astype(BF16)
        copies = []
        if it:
            scaled[it - 1] = own_scaled
            for device, side in both:
                copy = remote(
                    scaled.at[it - 1],
                    got_scaled.at[it - 1, side],
                    vec_send.at[it - 1, side],
                    vec_recv.at[it - 1, side],
                    device,
                )
                copy.start()
                copies.append(copy)
            sent_only.extend(copies)
        beside(0)
        if it:
            total = product(own_scaled, OO, 0, PTS)
        to_prev = product(own_scaled, OP, 0, PTS)
        beside(1)
        if it:
            for copy in copies:
                copy.wait_recv()
            from_prev, from_next = got_scaled[it - 1, 0], got_scaled[it - 1, 1]
        else:
            from_prev, from_next = scaled_start(0, inv_prev), scaled_start(1, inv_next)
        part_copies = []
        for half in range(2):
            at = pl.ds(half * HALF, HALF)
            for device, side in both:
                if side == 0:
                    piece = product(from_prev, PN, half * HALF, HALF)
                else:
                    piece = to_prev[:, half * HALF : (half + 1) * HALF]
                    piece = piece + product(from_next, NP, half * HALF, HALF)
                part[it, side, half] = piece.astype(PARTIAL)
                copy = remote(
                    part.at[it, side, half],
                    got_part.at[it, side, half],
                    part_send.at[it, side, half],
                    part_recv.at[it, side, half],
                    device,
                )
                copy.start()
                part_copies.append(copy)
        sent_only.extend(part_copies)
        if not it:
            total = product(own_scaled, OO, 0, PTS)
        total = total + product(from_prev, PO, 0, PTS)
        beside(2)
        beside(3)
        for copy in part_copies:
            copy.wait_recv()
        halves = [
            got_part[it, 0, half].astype(F32) + got_part[it, 1, half].astype(F32) for half in range(2)
        ]
        return (total + jnp.concatenate(halves, axis=1)) * inv_root

    scale = math.sqrt(n_row * n_col * PTS)
    image = apply_affinity(0, x_cols[...], no_beside)
    for it in range(1, ITERS):
        state = {}

        def beside(stage_index):
            if stage_index == 0:
                state["sum"] = gram_packed(image)
            else:
                state["sum"] = reduce_wait(it - 1, stage_index - 1, state["sum"], state["copies"])
            if stage_index < 3:
                state["copies"] = reduce_send(it - 1, stage_index, state["sum"])
            else:
                factors[it - 1] = inverse_factor(state["sum"]) * scale

        following = apply_affinity(it, image, beside)
        image = apply_factor(factors[it - 1], following)

    packed = gram_packed(image)
    for phase in range(3):
        copies = reduce_send(ITERS - 1, phase, packed)
        packed = reduce_wait(ITERS - 1, phase, packed, copies)
    result = apply_factor(inverse_factor(packed) * scale, image)
    out[...] = result

    for copy in pending + sent_only:
        copy.wait_send()


def on_device(n_row, n_col, embeddings, neighbour_ids, start_vectors):
    sums = n_row - 1 + n_col - 1 + 1
    n_chunks = len(CHUNKS) + len(SPLIT) - 1
    return pl.pallas_call(
        functools.partial(kernel, n_row, n_col),
        out_shape=jax.ShapeDtypeStruct((K, PTS), F32),
        in_specs=[
            pl.BlockSpec(memory_space=pl.ANY),
            pl.BlockSpec(memory_space=pl.ANY),
            pl.BlockSpec(memory_space=pl.ANY),
        ],
        out_specs=pl.BlockSpec(memory_space=pltpu.VMEM),
        scratch_shapes=[
            pltpu.VMEM((PTS, D), F32),
            pltpu.VMEM((3, PTS, D), BF16),
            pltpu.VMEM((5, PTS, PTS), BF16),
            pltpu.VMEM((K, PTS), F32),
            pltpu.VMEM((BLK_DEV, SLOTS), jnp.int32),
            pltpu.VMEM((8, 128), F32),
            pltpu.VMEM((2, 8, 128), F32),
            pltpu.VMEM((16, PTS), F32),
            pltpu.VMEM((3, 8, PTS), F32),
            pltpu.VMEM((3, 8, 128), F32),
            pltpu.VMEM((2, 2, 8, 128), F32),
            pltpu.VMEM((2, 8, 128), F32),
            pltpu.VMEM((K, PTS), BF16),
            pltpu.VMEM((2, K, PTS), BF16),
            pltpu.VMEM((ITERS - 1, K, K), F32),
            pltpu.VMEM((3, CHUNKS[-1][1], PTS), F32),
            pltpu.VMEM((3, PTS, CHUNKS[-1][1]), F32),
            pltpu.VMEM((ITERS, K // 2, 2 * K), F32),
            pltpu.VMEM((ITERS - 1, K, PTS), BF16),
            pltpu.VMEM((ITERS - 1, 2, K, PTS), BF16),
            pltpu.VMEM((ITERS, 2, 2, K, HALF), PARTIAL),
            pltpu.VMEM((ITERS, 2, 2, K, HALF), PARTIAL),
            pltpu.VMEM((ITERS, K // 2, 2 * K), F32),
            pltpu.VMEM((ITERS, K // 2 // CORES, 2 * K), F32),
            pltpu.VMEM((ITERS, sums, K // 2 // CORES, 2 * K), F32),
            pltpu.SemaphoreType.DMA((n_chunks,)),
            pltpu.SemaphoreType.DMA((2,)),
            pltpu.SemaphoreType.DMA((2, n_chunks)),
            pltpu.SemaphoreType.DMA((2, n_chunks)),
            pltpu.SemaphoreType.DMA((2,)),
            pltpu.SemaphoreType.DMA((2,)),
            pltpu.SemaphoreType.DMA((4,)),
            pltpu.SemaphoreType.DMA((4,)),
            pltpu.SemaphoreType.DMA((2,)),
            pltpu.SemaphoreType.DMA((2,)),
            pltpu.SemaphoreType.DMA((ITERS - 1, 2)),
            pltpu.SemaphoreType.DMA((ITERS - 1, 2)),
            pltpu.SemaphoreType.DMA((ITERS, 2, 2)),
            pltpu.SemaphoreType.DMA((ITERS, 2, 2)),
            pltpu.SemaphoreType.DMA((ITERS, sums)),
            pltpu.SemaphoreType.DMA((ITERS, sums)),
        ],
        compiler_params=pltpu.CompilerParams(
            collective_id=0, has_side_effects=True, vmem_limit_bytes=63 * 2**20
        ),
    )(embeddings, neighbour_ids, start_vectors.T).T


def solution(mesh):
    split = P(("row", "col"), None)
    return jax.shard_map(
        functools.partial(on_device, mesh.shape["row"], mesh.shape["col"]),
        mesh=mesh,
        in_specs=(split, split, split),
        out_specs=split,
        check_vma=False,
    )
```

```python
import functools
import math

import jax
import jax.numpy as jnp
from jax import lax
from jax.experimental import pallas as pl
from jax.experimental.pallas import tpu as pltpu
from jax.sharding import PartitionSpec as P

D = 1024
BS = 512
SLOTS = 12
K = 64
REACH = 2
ITERS = 3
BLK_DEV = 2
PTS = BS * BLK_DEV
SHARP = 8.0
EPSILON = 1e-06
CORES = 2
Z_CHIPS = 4
MESH = pl.DeviceIdType.MESH
BF16 = jnp.bfloat16
F32 = jnp.float32

CHUNKS = ((0, 256), (256, 256), (512, 256), (768, 256))
SPLIT = ((0, 512), (512, 256), (768, 256))
PARTIAL = BF16
HALF = PTS // 2
OO, PO, OP, NP, PN = range(5)
OWN, PREV, NEXT = range(3)


def split_hi_lo(x):
    hi = x.astype(BF16)
    return hi, (x - hi.astype(F32)).astype(BF16)


def gram_packed(image):
    hi, lo = split_hi_lo(image)
    both = jnp.concatenate([hi, lo], axis=0)
    full = lax.dot_general(both, both, (((1,), (1,)), ((), ())), preferred_element_type=F32)
    top = full[:K] + full[K:]
    gram = top[:, :K] + top[:, K:]
    return jnp.concatenate([gram[: K // 2], gram[K // 2 :]], axis=1)


def inverse_factor(packed):
    gram = jnp.concatenate([packed[:, :K], packed[:, K:]], axis=0)
    row_ids = lax.broadcasted_iota(jnp.int32, (K, K), 0)
    col_ids = lax.broadcasted_iota(jnp.int32, (K, K), 1)
    eye = jnp.where(row_ids == col_ids, 1.0, 0.0).astype(F32)
    work = jnp.concatenate([gram, eye], axis=1)
    in_group = lax.broadcasted_iota(jnp.int32, (8, 2 * K), 0)
    groups = [work[8 * g : 8 * g + 8] for g in range(K // 8)]

    def wide(value):
        return jnp.broadcast_to(value, (8, 2 * K))

    for k in range(0, K, 4):
        first, r = divmod(k, 8)
        head = groups[first]
        rows = [wide(head[r + i : r + i + 1]) for i in range(4)]
        p = {
            (i, j): wide(head[r + i : r + i + 1, k + j : k + j + 1])
            for i in range(4)
            for j in range(i, 4)
        }
        columns = [[wide(group[:, k + i : k + i + 1]) for i in range(4)] for group in groups[first:]]
        a, b, d = p[0, 0], p[0, 1], p[1, 1]
        inv_a = 1.0 / a
        inv_det = 1.0 / (a * d - b * b)
        d_, b_, a_ = d * inv_det, b * inv_det, a * inv_det
        w = {j: (d_ * p[0, j] - b_ * p[1, j], a_ * p[1, j] - b_ * p[0, j]) for j in (2, 3)}
        u0 = d_ * rows[0] - b_ * rows[1]
        u1 = a_ * rows[1] - b_ * rows[0]
        s22 = p[2, 2] - w[2][0] * p[0, 2] - w[2][1] * p[1, 2]
        s23 = p[2, 3] - w[2][0] * p[0, 3] - w[2][1] * p[1, 3]
        s33 = p[3, 3] - w[3][0] * p[0, 3] - w[3][1] * p[1, 3]
        inv_s22 = 1.0 / s22
        inv_rest = 1.0 / (s22 * s33 - s23 * s23)
        s2 = rows[2] - p[0, 2] * u0 - p[1, 2] * u1
        s3 = rows[3] - p[0, 3] * u0 - p[1, 3] * u1
        t2 = (s33 * inv_rest) * s2 - (s23 * inv_rest) * s3
        t3 = (s22 * inv_rest) * s3 - (s23 * inv_rest) * s2
        t0 = u0 - w[2][0] * t2 - w[3][0] * t3
        t1 = u1 - w[2][1] * t2 - w[3][1] * t3
        for g in range(first, K // 8):
            c = columns[g - first]
            below = groups[g]
            new = below - (c[0] * t0 + c[1] * t1) - (c[2] * t2 + c[3] * t3)
            if g == first:
                second = rows[1] - (b * inv_a) * rows[0]
                fourth = s3 - (s23 * inv_s22) * s2
                kept = jnp.where(in_group == r + 2, s2, jnp.where(in_group == r + 3, fourth, below))
                kept = jnp.where(in_group == r + 1, second, kept)
                new = jnp.where(in_group > r + 3, new, kept)
            groups[g] = new
    work = jnp.concatenate(groups, axis=0)
    pivots = jnp.sum(work[:, :K] * eye, axis=1, keepdims=True)
    return work[:, K:] * lax.rsqrt(pivots)


def folded(row):
    return jnp.concatenate([row[:, 128 * g : 128 * g + 128] for g in range(PTS // 128)], axis=0)


def unfolded(tile):
    return jnp.concatenate([tile[g : g + 1] for g in range(PTS // 128)], axis=1)


def apply_factor(inverse, image):
    mh, ml = split_hi_lo(inverse)
    zh, zl = split_hi_lo(image)
    left = jnp.concatenate([mh, mh, ml, ml], axis=1)
    right = jnp.concatenate([zh, zl, zh, zl], axis=0)
    return jnp.dot(left, right, preferred_element_type=F32)


def kernel(
    n_row, n_col,
    emb, ids_given, start, out,
    stage, normed, tiles, x_cols, ids, own_mask, got_mask, masks, deg, deg_sum, near_deg, far_deg,
    x_half, got_x, factors, wide, tall, whole_gram,
    scaled, got_scaled, part, got_part, gram, half_gram, got_gram,
    load_sem, x_sem, emb_send, emb_recv, mask_send, mask_recv, deg_send, deg_recv, start_send, start_recv,
    vec_send, vec_recv, part_send, part_recv, gram_send, gram_recv,
):
    row, col = lax.axis_index("row"), lax.axis_index("col")
    prev = (row, lax.rem(col + n_col - 1, n_col))
    nxt = (row, lax.rem(col + 1, n_col))
    n_y, n_x = n_row // CORES, n_col // Z_CHIPS
    y, core = row // CORES, lax.rem(row, CORES)
    x, z = col // Z_CHIPS, lax.rem(col, Z_CHIPS)
    def farthest_first(n_a, n_b):
        pairs = [(a, b) for a in range(n_a) for b in range(n_b) if a or b]
        return sorted(pairs, key=lambda s: -min(s[0], n_a - s[0]) - min(s[1], n_b - s[1]))

    steps = [farthest_first(n_y, CORES), farthest_first(n_x, Z_CHIPS), [(0, 1)]]
    other_core = (y * CORES + (1 - core), col)
    phases = [
        [(lax.rem(y + a, n_y) * CORES + lax.rem(core + b, CORES), col) for a, b in steps[0]],
        [(row, lax.rem(x + a, n_x) * Z_CHIPS + lax.rem(z + b, Z_CHIPS)) for a, b in steps[1]],
    ]
    mirror = [
        [steps[0].index((-a % n_y, -b % CORES)) for a, b in steps[0]],
        [steps[1].index((-a % n_x, -b % Z_CHIPS)) for a, b in steps[1]],
    ]
    base = [0, len(steps[0]), len(steps[0]) + len(steps[1])]
    part_rows = K // 2 // CORES

    def rows_of(which):
        return pl.ds(pl.multiple_of(which * part_rows, part_rows), part_rows)

    loads = []
    for i, (begin, count) in enumerate(CHUNKS):
        load = pltpu.make_async_copy(
            emb.at[pl.ds(begin, count)], stage.at[pl.ds(begin, count)], load_sem.at[i]
        )
        load.start()
        loads.append(load)
    x_load = pltpu.make_async_copy(start, x_cols, x_sem.at[0])
    x_load.start()
    ids_load = pltpu.make_async_copy(ids_given, ids, x_sem.at[1])
    ids_load.start()

    barrier = pltpu.get_barrier_semaphore()
    friends = [d for p in phases for d in p]
    for friend in friends:
        pl.semaphore_signal(barrier, inc=1, device_id=friend, device_id_type=MESH)

    lane = lax.broadcasted_iota(jnp.int32, (BLK_DEV, 128), 1)
    holder = col + (lane >> 1) - REACH
    holder = jnp.where(holder < 0, holder + n_col, jnp.where(holder >= n_col, holder - n_col, holder))
    target = (row * n_col + holder) * BLK_DEV + (lane & 1)
    me = (row * n_col + col) * BLK_DEV + lax.broadcasted_iota(jnp.int32, (BLK_DEV, 128), 0)
    ids_load.wait()
    count_listed = jnp.zeros((BLK_DEV, 128), F32)
    for slot in range(SLOTS):
        named = ids[:, slot : slot + 1]
        hit = named == target
        if slot:
            hit = hit & (named != me)
        count_listed += jnp.where(hit, 1.0, 0.0)
    own_mask[...] = jnp.zeros((8, 128), F32)
    own_mask[0:BLK_DEV, :] = count_listed

    def normalize(begin, count):
        step = 32

        def some(i, carry):
            rows = pl.ds(begin + i * step, step)
            e = stage[rows, :]
            inv = lax.rsqrt(jnp.mean(e * e, axis=-1, keepdims=True) + EPSILON)
            normed[OWN, rows, :] = (e * inv).astype(BF16)
            return carry

        lax.fori_loop(0, count // step, some, 0)

    def remote(src, dst, send, recv, device):
        return pltpu.make_async_remote_copy(
            src_ref=src, dst_ref=dst, send_sem=send, recv_sem=recv, device_id=device, device_id_type=MESH
        )

    both = ((nxt, 0), (prev, 1))
    moving = [[], []]
    start_copies = []
    mask_copies = []
    for i, (begin, count) in enumerate(CHUNKS):
        loads[i].wait()
        normalize(begin, count)
        if i == 0:
            pl.semaphore_wait(barrier, len(friends))
            for device, side in both:
                copy = remote(own_mask, got_mask.at[side], mask_send.at[side], mask_recv.at[side], device)
                copy.start()
                mask_copies.append(copy)
        rows = pl.ds(begin, count)
        for first, width in SPLIT if i == len(CHUNKS) - 1 else ((0, D),):
            for device, side in both:
                at = len(moving[side])
                copy = remote(
                    normed.at[OWN, rows, pl.ds(first, width)],
                    normed.at[PREV + side, rows, pl.ds(first, width)],
                    emb_send.at[side, at],
                    emb_recv.at[side, at],
                    device,
                )
                copy.start()
                moving[side].append(copy)
    x_load.wait()
    x_half[...] = x_cols[...].astype(BF16)
    for device, side in both:
        copy = remote(x_half, got_x.at[side], start_send.at[side], start_recv.at[side], device)
        copy.start()
        start_copies.append(copy)

    first_block = lax.broadcasted_iota(jnp.int32, (1, PTS), 1) < BS

    def spread_mask(tile, listing, candidate):
        for block in range(BLK_DEV):
            at = candidate + block
            masks[pl.ds(2 * tile + block, 1), :] = jnp.where(
                first_block, listing[0:1, at : at + 1], listing[1:2, at : at + 1]
            )

    def offset_at(offset):
        return (offset + REACH) * BLK_DEV

    left = {OO: OWN, PO: PREV, OP: OWN, NP: NEXT, PN: PREV}
    right = {OO: OWN, PO: OWN, OP: PREV, NP: PREV, PN: NEXT}

    def dots(tile, r0, r_count, c0, c_count, first=0, width=D):
        a = normed[left[tile], pl.ds(r0, r_count), pl.ds(first, width)]
        b = normed[right[tile], pl.ds(c0, c_count), pl.ds(first, width)]
        return lax.dot_general(a, b, (((1,), (1,)), ((), ())), preferred_element_type=F32)

    def affinity(tile, r0, r_count, c0, c_count, product=None):
        if product is None:
            product = dots(tile, r0, r_count, c0, c_count)
        value = jnp.exp(product * (SHARP / D) - SHARP)
        lists = [masks[pl.ds(2 * tile + block, 1), pl.ds(c0, c_count)] for block in range(BLK_DEV)]
        if r0 < BS < r0 + r_count:
            above = BS - r0
            value = jnp.concatenate([value[:above] * lists[0], value[above:] * lists[1]], axis=0)
        else:
            value = value * lists[r0 // BS]
        tiles[tile, pl.ds(r0, r_count), pl.ds(c0, c_count)] = value.astype(BF16)
        deg[right[tile], :, pl.ds(c0, c_count)] += jnp.sum(
            value.reshape(r_count // 8, 8, c_count), axis=0
        )

    deg[...] = jnp.zeros((3, 8, PTS), F32)
    mine = own_mask[...]
    spread_mask(OO, mine, offset_at(0))
    spread_mask(PO, mine, offset_at(-1))
    for begin, count in CHUNKS:
        affinity(OO, begin, count, 0, PTS)
    for copy in mask_copies:
        copy.wait()
    theirs = got_mask[0]
    spread_mask(OP, theirs, offset_at(1))
    spread_mask(NP, theirs, offset_at(2))
    spread_mask(PN, got_mask[1], offset_at(-2))

    for i, (begin, count) in enumerate(CHUNKS[:-1]):
        moving[0][i].wait_recv()
        affinity(PO, begin, count, 0, PTS)
        affinity(OP, 0, PTS, begin, count)
        moving[1][i].wait_recv()
        end = begin + count
        affinity(NP, begin, count, 0, end)
        affinity(PN, begin, count, 0, end)
        if begin:
            affinity(NP, 0, begin, begin, count)
            affinity(PN, 0, begin, begin, count)

    begin, count = CHUNKS[-1]
    last = len(CHUNKS) - 1
    blocks = (
        (PN, begin, count, 0, PTS, wide.at[2]),
        (PN, 0, begin, begin, count, tall.at[2, pl.ds(0, begin)]),
        (NP, begin, count, 0, PTS, wide.at[1]),
        (NP, 0, begin, begin, count, tall.at[1, pl.ds(0, begin)]),
        (OP, 0, PTS, begin, count, tall.at[0]),
        (PO, begin, count, 0, PTS, wide.at[0]),
    )
    for part_index, (first, width) in enumerate(SPLIT[:-1]):
        moving[0][last + part_index].wait_recv()
        moving[1][last + part_index].wait_recv()
        for tile, r0, r_count, c0, c_count, kept in blocks:
            partly = dots(tile, r0, r_count, c0, c_count, first, width)
            kept[...] = kept[...] + partly if part_index else partly

    far_prev = (row, lax.rem(col + n_col - 2, n_col))
    far_next = (row, lax.rem(col + 2, n_col))
    deg_copies = []

    def send_degrees(place, where, copies):
        deg_sum[place] = folded(jnp.sum(deg[where], axis=0, keepdims=True))
        for copy in copies:
            copy.start()
        deg_copies.extend(copies)

    moving[0][-1].wait_recv()
    moving[1][-1].wait_recv()
    for tile, r0, r_count, c0, c_count, kept in blocks:
        total = kept[...] + dots(tile, r0, r_count, c0, c_count, *SPLIT[-1])
        affinity(tile, r0, r_count, c0, c_count, total)
        if tile == PN and r0 == 0:
            send_degrees(
                2, NEXT, [remote(deg_sum.at[2], far_deg.at[0], deg_send.at[2], deg_recv.at[2], far_next)]
            )
        if tile == OP:
            send_degrees(
                0, PREV, [remote(deg_sum.at[0], far_deg.at[1], deg_send.at[3], deg_recv.at[3], far_prev)]
            )
    send_degrees(
        1,
        OWN,
        [
            remote(deg_sum.at[pl.ds(1, 2)], near_deg.at[0], deg_send.at[0], deg_recv.at[0], nxt),
            remote(deg_sum.at[pl.ds(0, 2)], near_deg.at[1], deg_send.at[1], deg_recv.at[1], prev),
        ],
    )
    for copy in start_copies + deg_copies:
        copy.wait_recv()
    inv_root = unfolded(lax.rsqrt(deg_sum[1] + near_deg[0, 1] + near_deg[1, 0]))
    inv_prev = unfolded(lax.rsqrt(deg_sum[0] + near_deg[0, 0] + far_deg[0]))
    inv_next = unfolded(lax.rsqrt(deg_sum[2] + near_deg[1, 1] + far_deg[1]))

    pending = deg_copies + start_copies + moving[0] + moving[1]
    sent_only = []

    def product(vectors, tile, c0, c_count):
        return jnp.dot(vectors, tiles[tile, :, pl.ds(c0, c_count)], preferred_element_type=F32)

    def reduce_send(it, phase, packed):
        copies = []
        if phase == 0:
            gram[it] = packed
            for k, device in enumerate(phases[0]):
                theirs = lax.rem(core + steps[0][k][1], CORES)
                copies.append((gram.at[it, rows_of(theirs)], got_gram, mirror[0][k], k, device))
        elif phase == 1:
            half_gram[it] = packed
            for k, device in enumerate(phases[1]):
                slot = base[1] + mirror[1][k]
                copies.append((half_gram.at[it], got_gram, slot, base[1] + k, device))
        else:
            whole_gram[it, rows_of(core), :] = packed
            mine = whole_gram.at[it, rows_of(core)]
            copies.append((mine, None, base[2], base[2], other_core))
        started = []
        for src, landing, slot, k, device in copies:
            dst = src if landing is None else landing.at[it, slot]
            copy = remote(src, dst, gram_send.at[it, k], gram_recv.at[it, slot], device)
            copy.start()
            started.append(copy)
        sent_only.extend(started)
        return started

    def reduce_wait(it, phase, packed, copies):
        for copy in copies:
            copy.wait_recv()
        if phase == 2:
            return whole_gram[it]
        if phase == 0:
            packed = gram[it, rows_of(core), :]
        for k in range(len(phases[phase])):
            packed = packed + got_gram[it, base[phase] + k]
        return packed

    def no_beside(stage_index):
        return None

    def scaled_start(side, inverse):
        return (got_x[side].astype(F32) * inverse).astype(BF16)

    def apply_affinity(it, vectors, beside):
        own_scaled = (vectors * inv_root).astype(BF16)
        copies = []
        if it:
            scaled[it - 1] = own_scaled
            for device, side in both:
                copy = remote(
                    scaled.at[it - 1],
                    got_scaled.at[it - 1, side],
                    vec_send.at[it - 1, side],
                    vec_recv.at[it - 1, side],
                    device,
                )
                copy.start()
                copies.append(copy)
            sent_only.extend(copies)
        beside(0)
        if it:
            total = product(own_scaled, OO, 0, PTS)
        to_prev = product(own_scaled, OP, 0, PTS)
        beside(1)
        if it:
            for copy in copies:
                copy.wait_recv()
            from_prev, from_next = got_scaled[it - 1, 0], got_scaled[it - 1, 1]
        else:
            from_prev, from_next = scaled_start(0, inv_prev), scaled_start(1, inv_next)
        part_copies = []
        for half in range(2):
            at = pl.ds(half * HALF, HALF)
            for device, side in both:
                if side == 0:
                    piece = product(from_prev, PN, half * HALF, HALF)
                else:
                    piece = to_prev[:, half * HALF : (half + 1) * HALF]
                    piece = piece + product(from_next, NP, half * HALF, HALF)
                part[it, side, half] = piece.astype(PARTIAL)
                copy = remote(
                    part.at[it, side, half],
                    got_part.at[it, side, half],
                    part_send.at[it, side, half],
                    part_recv.at[it, side, half],
                    device,
                )
                copy.start()
                part_copies.append(copy)
        sent_only.extend(part_copies)
        if not it:
            total = product(own_scaled, OO, 0, PTS)
        total = total + product(from_prev, PO, 0, PTS)
        beside(2)
        beside(3)
        for copy in part_copies:
            copy.wait_recv()
        halves = [
            got_part[it, 0, half].astype(F32) + got_part[it, 1, half].astype(F32) for half in range(2)
        ]
        return (total + jnp.concatenate(halves, axis=1)) * inv_root

    scale = math.sqrt(n_row * n_col * PTS)
    image = apply_affinity(0, x_cols[...], no_beside)
    for it in range(1, ITERS):
        state = {}

        def beside(stage_index):
            if stage_index == 0:
                state["sum"] = gram_packed(image)
            else:
                state["sum"] = reduce_wait(it - 1, stage_index - 1, state["sum"], state["copies"])
            if stage_index < 3:
                state["copies"] = reduce_send(it - 1, stage_index, state["sum"])
            else:
                factors[it - 1] = inverse_factor(state["sum"]) * scale

        following = apply_affinity(it, image, beside)
        image = apply_factor(factors[it - 1], following)

    packed = gram_packed(image)
    for phase in range(3):
        copies = reduce_send(ITERS - 1, phase, packed)
        packed = reduce_wait(ITERS - 1, phase, packed, copies)
    result = apply_factor(inverse_factor(packed) * scale, image)
    out[...] = result

    for copy in pending + sent_only:
        copy.wait_send()


def on_device(n_row, n_col, embeddings, neighbour_ids, start_vectors):
    sums = n_row - 1 + n_col - 1 + 1
    n_chunks = len(CHUNKS) + len(SPLIT) - 1
    return pl.pallas_call(
        functools.partial(kernel, n_row, n_col),
        out_shape=jax.ShapeDtypeStruct((K, PTS), F32),
        in_specs=[
            pl.BlockSpec(memory_space=pl.ANY),
            pl.BlockSpec(memory_space=pl.ANY),
            pl.BlockSpec(memory_space=pl.ANY),
        ],
        out_specs=pl.BlockSpec(memory_space=pltpu.VMEM),
        scratch_shapes=[
            pltpu.VMEM((PTS, D), F32),
            pltpu.VMEM((3, PTS, D), BF16),
            pltpu.VMEM((5, PTS, PTS), BF16),
            pltpu.VMEM((K, PTS), F32),
            pltpu.VMEM((BLK_DEV, SLOTS), jnp.int32),
            pltpu.VMEM((8, 128), F32),
            pltpu.VMEM((2, 8, 128), F32),
            pltpu.VMEM((16, PTS), F32),
            pltpu.VMEM((3, 8, PTS), F32),
            pltpu.VMEM((3, 8, 128), F32),
            pltpu.VMEM((2, 2, 8, 128), F32),
            pltpu.VMEM((2, 8, 128), F32),
            pltpu.VMEM((K, PTS), BF16),
            pltpu.VMEM((2, K, PTS), BF16),
            pltpu.VMEM((ITERS - 1, K, K), F32),
            pltpu.VMEM((3, CHUNKS[-1][1], PTS), F32),
            pltpu.VMEM((3, PTS, CHUNKS[-1][1]), F32),
            pltpu.VMEM((ITERS, K // 2, 2 * K), F32),
            pltpu.VMEM((ITERS - 1, K, PTS), BF16),
            pltpu.VMEM((ITERS - 1, 2, K, PTS), BF16),
            pltpu.VMEM((ITERS, 2, 2, K, HALF), PARTIAL),
            pltpu.VMEM((ITERS, 2, 2, K, HALF), PARTIAL),
            pltpu.VMEM((ITERS, K // 2, 2 * K), F32),
            pltpu.VMEM((ITERS, K // 2 // CORES, 2 * K), F32),
            pltpu.VMEM((ITERS, sums, K // 2 // CORES, 2 * K), F32),
            pltpu.SemaphoreType.DMA((n_chunks,)),
            pltpu.SemaphoreType.DMA((2,)),
            pltpu.SemaphoreType.DMA((2, n_chunks)),
            pltpu.SemaphoreType.DMA((2, n_chunks)),
            pltpu.SemaphoreType.DMA((2,)),
            pltpu.SemaphoreType.DMA((2,)),
            pltpu.SemaphoreType.DMA((4,)),
            pltpu.SemaphoreType.DMA((4,)),
            pltpu.SemaphoreType.DMA((2,)),
            pltpu.SemaphoreType.DMA((2,)),
            pltpu.SemaphoreType.DMA((ITERS - 1, 2)),
            pltpu.SemaphoreType.DMA((ITERS - 1, 2)),
            pltpu.SemaphoreType.DMA((ITERS, 2, 2)),
            pltpu.SemaphoreType.DMA((ITERS, 2, 2)),
            pltpu.SemaphoreType.DMA((ITERS, sums)),
            pltpu.SemaphoreType.DMA((ITERS, sums)),
        ],
        compiler_params=pltpu.CompilerParams(
            collective_id=0, has_side_effects=True, vmem_limit_bytes=63 * 2**20
        ),
    )(embeddings, neighbour_ids, start_vectors.T).T


def solution(mesh):
    split = P(("row", "col"), None)
    return jax.shard_map(
        functools.partial(on_device, mesh.shape["row"], mesh.shape["col"]),
        mesh=mesh,
        in_specs=(split, split, split),
        out_specs=split,
        check_vma=False,
    )
```

```python
import functools
import math

import jax
import jax.numpy as jnp
from jax import lax
from jax.experimental import pallas as pl
from jax.experimental.pallas import tpu as pltpu
from jax.sharding import PartitionSpec as P

D = 1024
BS = 512
SLOTS = 12
K = 64
REACH = 2
ITERS = 3
BLK_DEV = 2
PTS = BS * BLK_DEV
SHARP = 8.0
EPSILON = 1e-06
CORES = 2
Z_CHIPS = 4
MESH = pl.DeviceIdType.MESH
BF16 = jnp.bfloat16
F32 = jnp.float32

CHUNKS = ((0, 256), (256, 256), (512, 256), (768, 256))
SPLIT = ((0, 512), (512, 256), (768, 256))
PARTIAL = BF16
HALF = PTS // 2
OO, PO, OP, NP, PN = range(5)
OWN, PREV, NEXT = range(3)


def split_hi_lo(x):
    hi = x.astype(BF16)
    return hi, (x - hi.astype(F32)).astype(BF16)


def gram_packed(image):
    hi, lo = split_hi_lo(image)
    both = jnp.concatenate([hi, lo], axis=0)
    full = lax.dot_general(both, both, (((1,), (1,)), ((), ())), preferred_element_type=F32)
    top = full[:K] + full[K:]
    gram = top[:, :K] + top[:, K:]
    return jnp.concatenate([gram[: K // 2], gram[K // 2 :]], axis=1)


def inverse_factor(packed):
    gram = jnp.concatenate([packed[:, :K], packed[:, K:]], axis=0)
    row_ids = lax.broadcasted_iota(jnp.int32, (K, K), 0)
    col_ids = lax.broadcasted_iota(jnp.int32, (K, K), 1)
    eye = jnp.where(row_ids == col_ids, 1.0, 0.0).astype(F32)
    work = jnp.concatenate([gram, eye], axis=1)
    in_group = lax.broadcasted_iota(jnp.int32, (8, 2 * K), 0)
    groups = [work[8 * g : 8 * g + 8] for g in range(K // 8)]

    def wide(value):
        return jnp.broadcast_to(value, (8, 2 * K))

    for k in range(0, K, 4):
        first, r = divmod(k, 8)
        head = groups[first]
        rows = [wide(head[r + i : r + i + 1]) for i in range(4)]
        p = {
            (i, j): wide(head[r + i : r + i + 1, k + j : k + j + 1])
            for i in range(4)
            for j in range(i, 4)
        }
        columns = [[wide(group[:, k + i : k + i + 1]) for i in range(4)] for group in groups[first:]]
        a, b, d = p[0, 0], p[0, 1], p[1, 1]
        inv_a = 1.0 / a
        inv_det = 1.0 / (a * d - b * b)
        d_, b_, a_ = d * inv_det, b * inv_det, a * inv_det
        w = {j: (d_ * p[0, j] - b_ * p[1, j], a_ * p[1, j] - b_ * p[0, j]) for j in (2, 3)}
        u0 = d_ * rows[0] - b_ * rows[1]
        u1 = a_ * rows[1] - b_ * rows[0]
        s22 = p[2, 2] - w[2][0] * p[0, 2] - w[2][1] * p[1, 2]
        s23 = p[2, 3] - w[2][0] * p[0, 3] - w[2][1] * p[1, 3]
        s33 = p[3, 3] - w[3][0] * p[0, 3] - w[3][1] * p[1, 3]
        inv_s22 = 1.0 / s22
        inv_rest = 1.0 / (s22 * s33 - s23 * s23)
        s2 = rows[2] - p[0, 2] * u0 - p[1, 2] * u1
        s3 = rows[3] - p[0, 3] * u0 - p[1, 3] * u1
        t2 = (s33 * inv_rest) * s2 - (s23 * inv_rest) * s3
        t3 = (s22 * inv_rest) * s3 - (s23 * inv_rest) * s2
        t0 = u0 - w[2][0] * t2 - w[3][0] * t3
        t1 = u1 - w[2][1] * t2 - w[3][1] * t3
        for g in range(first, K // 8):
            c = columns[g - first]
            below = groups[g]
            new = below - (c[0] * t0 + c[1] * t1) - (c[2] * t2 + c[3] * t3)
            if g == first:
                second = rows[1] - (b * inv_a) * rows[0]
                fourth = s3 - (s23 * inv_s22) * s2
                kept = jnp.where(in_group == r + 2, s2, jnp.where(in_group == r + 3, fourth, below))
                kept = jnp.where(in_group == r + 1, second, kept)
                new = jnp.where(in_group > r + 3, new, kept)
            groups[g] = new
    work = jnp.concatenate(groups, axis=0)
    pivots = jnp.sum(work[:, :K] * eye, axis=1, keepdims=True)
    return work[:, K:] * lax.rsqrt(pivots)


def folded(row):
    return jnp.concatenate([row[:, 128 * g : 128 * g + 128] for g in range(PTS // 128)], axis=0)


def unfolded(tile):
    return jnp.concatenate([tile[g : g + 1] for g in range(PTS // 128)], axis=1)


def apply_factor(inverse, image):
    mh, ml = split_hi_lo(inverse)
    zh, zl = split_hi_lo(image)
    left = jnp.concatenate([mh, mh, ml, ml], axis=1)
    right = jnp.concatenate([zh, zl, zh, zl], axis=0)
    return jnp.dot(left, right, preferred_element_type=F32)


def kernel(
    n_row, n_col,
    emb, ids_given, start, out,
    stage, normed, tiles, x_cols, ids, own_mask, got_mask, masks, deg, deg_sum, near_deg, far_deg,
    x_half, got_x, factors, wide, tall, whole_gram,
    scaled, got_scaled, part, got_part, gram, half_gram, got_gram,
    load_sem, x_sem, emb_send, emb_recv, mask_send, mask_recv, deg_send, deg_recv, start_send, start_recv,
    vec_send, vec_recv, part_send, part_recv, gram_send, gram_recv,
):
    row, col = lax.axis_index("row"), lax.axis_index("col")
    prev = (row, lax.rem(col + n_col - 1, n_col))
    nxt = (row, lax.rem(col + 1, n_col))
    n_y, n_x = n_row // CORES, n_col // Z_CHIPS
    y, core = row // CORES, lax.rem(row, CORES)
    x, z = col // Z_CHIPS, lax.rem(col, Z_CHIPS)
    def farthest_first(n_a, n_b):
        pairs = [(a, b) for a in range(n_a) for b in range(n_b) if a or b]
        return sorted(pairs, key=lambda s: -min(s[0], n_a - s[0]) - min(s[1], n_b - s[1]))

    steps = [farthest_first(n_y, CORES), farthest_first(n_x, Z_CHIPS), [(0, 1)]]
    other_core = (y * CORES + (1 - core), col)
    phases = [
        [(lax.rem(y + a, n_y) * CORES + lax.rem(core + b, CORES), col) for a, b in steps[0]],
        [(row, lax.rem(x + a, n_x) * Z_CHIPS + lax.rem(z + b, Z_CHIPS)) for a, b in steps[1]],
    ]
    mirror = [
        [steps[0].index((-a % n_y, -b % CORES)) for a, b in steps[0]],
        [steps[1].index((-a % n_x, -b % Z_CHIPS)) for a, b in steps[1]],
    ]
    base = [0, len(steps[0]), len(steps[0]) + len(steps[1])]
    part_rows = K // 2 // CORES

    def rows_of(which):
        return pl.ds(pl.multiple_of(which * part_rows, part_rows), part_rows)

    loads = []
    for i, (begin, count) in enumerate(CHUNKS):
        load = pltpu.make_async_copy(
            emb.at[pl.ds(begin, count)], stage.at[pl.ds(begin, count)], load_sem.at[i]
        )
        load.start()
        loads.append(load)
    x_load = pltpu.make_async_copy(start, x_cols, x_sem.at[0])
    x_load.start()
    ids_load = pltpu.make_async_copy(ids_given, ids, x_sem.at[1])
    ids_load.start()

    barrier = pltpu.get_barrier_semaphore()
    friends = [d for p in phases for d in p]
    for friend in friends:
        pl.semaphore_signal(barrier, inc=1, device_id=friend, device_id_type=MESH)

    lane = lax.broadcasted_iota(jnp.int32, (BLK_DEV, 128), 1)
    holder = col + (lane >> 1) - REACH
    holder = jnp.where(holder < 0, holder + n_col, jnp.where(holder >= n_col, holder - n_col, holder))
    target = (row * n_col + holder) * BLK_DEV + (lane & 1)
    me = (row * n_col + col) * BLK_DEV + lax.broadcasted_iota(jnp.int32, (BLK_DEV, 128), 0)
    ids_load.wait()
    count_listed = jnp.zeros((BLK_DEV, 128), F32)
    for slot in range(SLOTS):
        named = ids[:, slot : slot + 1]
        hit = named == target
        if slot:
            hit = hit & (named != me)
        count_listed += jnp.where(hit, 1.0, 0.0)
    own_mask[...] = jnp.zeros((8, 128), F32)
    own_mask[0:BLK_DEV, :] = count_listed

    def normalize(begin, count):
        step = 32

        def some(i, carry):
            rows = pl.ds(begin + i * step, step)
            e = stage[rows, :]
            inv = lax.rsqrt(jnp.mean(e * e, axis=-1, keepdims=True) + EPSILON)
            normed[OWN, rows, :] = (e * inv).astype(BF16)
            return carry

        lax.fori_loop(0, count // step, some, 0)

    def remote(src, dst, send, recv, device):
        return pltpu.make_async_remote_copy(
            src_ref=src, dst_ref=dst, send_sem=send, recv_sem=recv, device_id=device, device_id_type=MESH
        )

    both = ((nxt, 0), (prev, 1))
    moving = [[], []]
    start_copies = []
    mask_copies = []
    for i, (begin, count) in enumerate(CHUNKS):
        loads[i].wait()
        normalize(begin, count)
        if i == 0:
            pl.semaphore_wait(barrier, len(friends))
            for device, side in both:
                copy = remote(own_mask, got_mask.at[side], mask_send.at[side], mask_recv.at[side], device)
                copy.start()
                mask_copies.append(copy)
        rows = pl.ds(begin, count)
        for first, width in SPLIT if i == len(CHUNKS) - 1 else ((0, D),):
            for device, side in both:
                at = len(moving[side])
                copy = remote(
                    normed.at[OWN, rows, pl.ds(first, width)],
                    normed.at[PREV + side, rows, pl.ds(first, width)],
                    emb_send.at[side, at],
                    emb_recv.at[side, at],
                    device,
                )
                copy.start()
                moving[side].append(copy)
    x_load.wait()
    x_half[...] = x_cols[...].astype(BF16)
    for device, side in both:
        copy = remote(x_half, got_x.at[side], start_send.at[side], start_recv.at[side], device)
        copy.start()
        start_copies.append(copy)

    first_block = lax.broadcasted_iota(jnp.int32, (1, PTS), 1) < BS

    def spread_mask(tile, listing, candidate):
        for block in range(BLK_DEV):
            at = candidate + block
            masks[pl.ds(2 * tile + block, 1), :] = jnp.where(
                first_block, listing[0:1, at : at + 1], listing[1:2, at : at + 1]
            )

    def offset_at(offset):
        return (offset + REACH) * BLK_DEV

    left = {OO: OWN, PO: PREV, OP: OWN, NP: NEXT, PN: PREV}
    right = {OO: OWN, PO: OWN, OP: PREV, NP: PREV, PN: NEXT}

    def dots(tile, r0, r_count, c0, c_count, first=0, width=D):
        a = normed[left[tile], pl.ds(r0, r_count), pl.ds(first, width)]
        b = normed[right[tile], pl.ds(c0, c_count), pl.ds(first, width)]
        return lax.dot_general(a, b, (((1,), (1,)), ((), ())), preferred_element_type=F32)

    def affinity(tile, r0, r_count, c0, c_count, product=None):
        if product is None:
            product = dots(tile, r0, r_count, c0, c_count)
        value = jnp.exp(product * (SHARP / D) - SHARP)
        lists = [masks[pl.ds(2 * tile + block, 1), pl.ds(c0, c_count)] for block in range(BLK_DEV)]
        if r0 < BS < r0 + r_count:
            above = BS - r0
            value = jnp.concatenate([value[:above] * lists[0], value[above:] * lists[1]], axis=0)
        else:
            value = value * lists[r0 // BS]
        tiles[tile, pl.ds(r0, r_count), pl.ds(c0, c_count)] = value.astype(BF16)
        deg[right[tile], :, pl.ds(c0, c_count)] += jnp.sum(
            value.reshape(r_count // 8, 8, c_count), axis=0
        )

    deg[...] = jnp.zeros((3, 8, PTS), F32)
    mine = own_mask[...]
    spread_mask(OO, mine, offset_at(0))
    spread_mask(PO, mine, offset_at(-1))
    for begin, count in CHUNKS:
        affinity(OO, begin, count, 0, PTS)
    for copy in mask_copies:
        copy.wait()
    theirs = got_mask[0]
    spread_mask(OP, theirs, offset_at(1))
    spread_mask(NP, theirs, offset_at(2))
    spread_mask(PN, got_mask[1], offset_at(-2))

    for i, (begin, count) in enumerate(CHUNKS[:-1]):
        moving[0][i].wait_recv()
        affinity(PO, begin, count, 0, PTS)
        affinity(OP, 0, PTS, begin, count)
        moving[1][i].wait_recv()
        end = begin + count
        affinity(NP, begin, count, 0, end)
        affinity(PN, begin, count, 0, end)
        if begin:
            affinity(NP, 0, begin, begin, count)
            affinity(PN, 0, begin, begin, count)

    begin, count = CHUNKS[-1]
    last = len(CHUNKS) - 1
    blocks = (
        (PN, begin, count, 0, PTS, wide.at[2]),
        (PN, 0, begin, begin, count, tall.at[2, pl.ds(0, begin)]),
        (NP, begin, count, 0, PTS, wide.at[1]),
        (NP, 0, begin, begin, count, tall.at[1, pl.ds(0, begin)]),
        (OP, 0, PTS, begin, count, tall.at[0]),
        (PO, begin, count, 0, PTS, wide.at[0]),
    )
    for part_index, (first, width) in enumerate(SPLIT[:-1]):
        moving[0][last + part_index].wait_recv()
        moving[1][last + part_index].wait_recv()
        for tile, r0, r_count, c0, c_count, kept in blocks:
            partly = dots(tile, r0, r_count, c0, c_count, first, width)
            kept[...] = kept[...] + partly if part_index else partly

    far_prev = (row, lax.rem(col + n_col - 2, n_col))
    far_next = (row, lax.rem(col + 2, n_col))
    deg_copies = []

    def send_degrees(place, where, copies):
        deg_sum[place] = folded(jnp.sum(deg[where], axis=0, keepdims=True))
        for copy in copies:
            copy.start()
        deg_copies.extend(copies)

    moving[0][-1].wait_recv()
    moving[1][-1].wait_recv()
    for tile, r0, r_count, c0, c_count, kept in blocks:
        total = kept[...] + dots(tile, r0, r_count, c0, c_count, *SPLIT[-1])
        affinity(tile, r0, r_count, c0, c_count, total)
        if tile == PN and r0 == 0:
            send_degrees(
                2, NEXT, [remote(deg_sum.at[2], far_deg.at[0], deg_send.at[2], deg_recv.at[2], far_next)]
            )
        if tile == OP:
            send_degrees(
                0, PREV, [remote(deg_sum.at[0], far_deg.at[1], deg_send.at[3], deg_recv.at[3], far_prev)]
            )
    send_degrees(
        1,
        OWN,
        [
            remote(deg_sum.at[pl.ds(1, 2)], near_deg.at[0], deg_send.at[0], deg_recv.at[0], nxt),
            remote(deg_sum.at[pl.ds(0, 2)], near_deg.at[1], deg_send.at[1], deg_recv.at[1], prev),
        ],
    )
    for copy in start_copies + deg_copies:
        copy.wait_recv()
    inv_root = unfolded(lax.rsqrt(deg_sum[1] + near_deg[0, 1] + near_deg[1, 0]))
    inv_prev = unfolded(lax.rsqrt(deg_sum[0] + near_deg[0, 0] + far_deg[0]))
    inv_next = unfolded(lax.rsqrt(deg_sum[2] + near_deg[1, 1] + far_deg[1]))

    pending = deg_copies + start_copies + moving[0] + moving[1]
    sent_only = []

    def product(vectors, tile, c0, c_count):
        return jnp.dot(vectors, tiles[tile, :, pl.ds(c0, c_count)], preferred_element_type=F32)

    def reduce_send(it, phase, packed):
        copies = []
        if phase == 0:
            gram[it] = packed
            for k, device in enumerate(phases[0]):
                theirs = lax.rem(core + steps[0][k][1], CORES)
                copies.append((gram.at[it, rows_of(theirs)], got_gram, mirror[0][k], k, device))
        elif phase == 1:
            half_gram[it] = packed
            for k, device in enumerate(phases[1]):
                slot = base[1] + mirror[1][k]
                copies.append((half_gram.at[it], got_gram, slot, base[1] + k, device))
        else:
            whole_gram[it, rows_of(core), :] = packed
            mine = whole_gram.at[it, rows_of(core)]
            copies.append((mine, None, base[2], base[2], other_core))
        started = []
        for src, landing, slot, k, device in copies:
            dst = src if landing is None else landing.at[it, slot]
            copy = remote(src, dst, gram_send.at[it, k], gram_recv.at[it, slot], device)
            copy.start()
            started.append(copy)
        sent_only.extend(started)
        return started

    def reduce_wait(it, phase, packed, copies):
        for copy in copies:
            copy.wait_recv()
        if phase == 2:
            return whole_gram[it]
        if phase == 0:
            packed = gram[it, rows_of(core), :]
        for k in range(len(phases[phase])):
            packed = packed + got_gram[it, base[phase] + k]
        return packed

    def no_beside(stage_index):
        return None

    def scaled_start(side, inverse):
        return (got_x[side].astype(F32) * inverse).astype(BF16)

    def apply_affinity(it, vectors, beside):
        own_scaled = (vectors * inv_root).astype(BF16)
        copies = []
        if it:
            scaled[it - 1] = own_scaled
            for device, side in both:
                copy = remote(
                    scaled.at[it - 1],
                    got_scaled.at[it - 1, side],
                    vec_send.at[it - 1, side],
                    vec_recv.at[it - 1, side],
                    device,
                )
                copy.start()
                copies.append(copy)
            sent_only.extend(copies)
        beside(0)
        if it:
            total = product(own_scaled, OO, 0, PTS)
            to_prev = product(own_scaled, OP, 0, PTS)
        beside(1)
        if it:
            for copy in copies:
                copy.wait_recv()
            from_prev, from_next = got_scaled[it - 1, 0], got_scaled[it - 1, 1]
        else:
            from_prev, from_next = scaled_start(0, inv_prev), scaled_start(1, inv_next)
        part_copies = []
        for half in range(2):
            at = pl.ds(half * HALF, HALF)
            for device, side in both:
                if side == 0:
                    piece = product(from_prev, PN, half * HALF, HALF)
                else:
                    if it:
                        piece = to_prev[:, half * HALF : (half + 1) * HALF]
                    else:
                        piece = product(own_scaled, OP, half * HALF, HALF)
                    piece = piece + product(from_next, NP, half * HALF, HALF)
                part[it, side, half] = piece.astype(PARTIAL)
                copy = remote(
                    part.at[it, side, half],
                    got_part.at[it, side, half],
                    part_send.at[it, side, half],
                    part_recv.at[it, side, half],
                    device,
                )
                copy.start()
                part_copies.append(copy)
        sent_only.extend(part_copies)
        if not it:
            total = product(own_scaled, OO, 0, PTS)
        total = total + product(from_prev, PO, 0, PTS)
        beside(2)
        beside(3)
        for copy in part_copies:
            copy.wait_recv()
        halves = [
            got_part[it, 0, half].astype(F32) + got_part[it, 1, half].astype(F32) for half in range(2)
        ]
        return (total + jnp.concatenate(halves, axis=1)) * inv_root

    scale = math.sqrt(n_row * n_col * PTS)
    image = apply_affinity(0, x_cols[...], no_beside)
    for it in range(1, ITERS):
        state = {}

        def beside(stage_index):
            if stage_index == 0:
                state["sum"] = gram_packed(image)
            else:
                state["sum"] = reduce_wait(it - 1, stage_index - 1, state["sum"], state["copies"])
            if stage_index < 3:
                state["copies"] = reduce_send(it - 1, stage_index, state["sum"])
            else:
                factors[it - 1] = inverse_factor(state["sum"]) * scale

        following = apply_affinity(it, image, beside)
        image = apply_factor(factors[it - 1], following)

    packed = gram_packed(image)
    for phase in range(3):
        copies = reduce_send(ITERS - 1, phase, packed)
        packed = reduce_wait(ITERS - 1, phase, packed, copies)
    result = apply_factor(inverse_factor(packed) * scale, image)
    out[...] = result

    for copy in pending + sent_only:
        copy.wait_send()


def on_device(n_row, n_col, embeddings, neighbour_ids, start_vectors):
    sums = n_row - 1 + n_col - 1 + 1
    n_chunks = len(CHUNKS) + len(SPLIT) - 1
    return pl.pallas_call(
        functools.partial(kernel, n_row, n_col),
        out_shape=jax.ShapeDtypeStruct((K, PTS), F32),
        in_specs=[
            pl.BlockSpec(memory_space=pl.ANY),
            pl.BlockSpec(memory_space=pl.ANY),
            pl.BlockSpec(memory_space=pl.ANY),
        ],
        out_specs=pl.BlockSpec(memory_space=pltpu.VMEM),
        scratch_shapes=[
            pltpu.VMEM((PTS, D), F32),
            pltpu.VMEM((3, PTS, D), BF16),
            pltpu.VMEM((5, PTS, PTS), BF16),
            pltpu.VMEM((K, PTS), F32),
            pltpu.VMEM((BLK_DEV, SLOTS), jnp.int32),
            pltpu.VMEM((8, 128), F32),
            pltpu.VMEM((2, 8, 128), F32),
            pltpu.VMEM((16, PTS), F32),
            pltpu.VMEM((3, 8, PTS), F32),
            pltpu.VMEM((3, 8, 128), F32),
            pltpu.VMEM((2, 2, 8, 128), F32),
            pltpu.VMEM((2, 8, 128), F32),
            pltpu.VMEM((K, PTS), BF16),
            pltpu.VMEM((2, K, PTS), BF16),
            pltpu.VMEM((ITERS - 1, K, K), F32),
            pltpu.VMEM((3, CHUNKS[-1][1], PTS), F32),
            pltpu.VMEM((3, PTS, CHUNKS[-1][1]), F32),
            pltpu.VMEM((ITERS, K // 2, 2 * K), F32),
            pltpu.VMEM((ITERS - 1, K, PTS), BF16),
            pltpu.VMEM((ITERS - 1, 2, K, PTS), BF16),
            pltpu.VMEM((ITERS, 2, 2, K, HALF), PARTIAL),
            pltpu.VMEM((ITERS, 2, 2, K, HALF), PARTIAL),
            pltpu.VMEM((ITERS, K // 2, 2 * K), F32),
            pltpu.VMEM((ITERS, K // 2 // CORES, 2 * K), F32),
            pltpu.VMEM((ITERS, sums, K // 2 // CORES, 2 * K), F32),
            pltpu.SemaphoreType.DMA((n_chunks,)),
            pltpu.SemaphoreType.DMA((2,)),
            pltpu.SemaphoreType.DMA((2, n_chunks)),
            pltpu.SemaphoreType.DMA((2, n_chunks)),
            pltpu.SemaphoreType.DMA((2,)),
            pltpu.SemaphoreType.DMA((2,)),
            pltpu.SemaphoreType.DMA((4,)),
            pltpu.SemaphoreType.DMA((4,)),
            pltpu.SemaphoreType.DMA((2,)),
            pltpu.SemaphoreType.DMA((2,)),
            pltpu.SemaphoreType.DMA((ITERS - 1, 2)),
            pltpu.SemaphoreType.DMA((ITERS - 1, 2)),
            pltpu.SemaphoreType.DMA((ITERS, 2, 2)),
            pltpu.SemaphoreType.DMA((ITERS, 2, 2)),
            pltpu.SemaphoreType.DMA((ITERS, sums)),
            pltpu.SemaphoreType.DMA((ITERS, sums)),
        ],
        compiler_params=pltpu.CompilerParams(
            collective_id=0, has_side_effects=True, vmem_limit_bytes=63 * 2**20
        ),
    )(embeddings, neighbour_ids, start_vectors.T).T


def solution(mesh):
    split = P(("row", "col"), None)
    return jax.shard_map(
        functools.partial(on_device, mesh.shape["row"], mesh.shape["col"]),
        mesh=mesh,
        in_specs=(split, split, split),
        out_specs=split,
        check_vma=False,
    )
```
